128 devices in a mesh: lon: 16 (over z_lo, y, core), lat: 4 (over x), ch: 2 (over z_hi).
Axes of the slice: x: 4, y: 4, z: 4 (z_hi: 2, z_lo: 2; z = z_hi * 2 + z_lo), core: 2. Of those that a mesh axis runs over, the one named last changes fastest.
Arguments:
- latents: bfloat16 [4, 64, 64, 2048], P(None, 'ch', 'lat', 'lon'), may hold values from -6 to 6
- conv_weight: bfloat16 [64, 27, 64], P('ch'), may hold values from -0.15625 to 0.15625
- gdn_gamma: float32 [64, 32], P('ch'), may hold values from 0 to 0.1
- gdn_beta: float32 [64], P('ch'), may hold values from 0.5 to 2
- hidden_weight: bfloat16 [128, 640], replicated, may hold values from -0.5 to 0.5
- hidden_bias: float32 [640], replicated, may hold values from -3 to 3
- param_weight: bfloat16 [640, 256], replicated, may hold values from -0.25 to 0.25
- param_bias: float32 [256], replicated, may hold values from -3 to 3
Outputs:
- conv_grad: float32 [64, 1728], P('ch', ('lon', 'lat'))
- hidden_weight_grad: float32 [128, 640], replicated
- hidden_bias_grad: float32 [640], replicated
- param_weight_grad: float32 [640, 256], replicated
- param_bias_grad: float32 [256], replicated
The draws below stay inside these ranges and needn't reach their ends.
All inputs are finite; a program needn't handle non-finite values.
Results may differ from the reference program's by a relative error of at most 0.0015.
Values may be sent and summed in bfloat16 or wider, within the bound.
A program may use at most 128 MiB of HBM per device.

```python
import math
import jax
import jax.numpy as jnp
from jax import lax

C = 64
GROUPS = 2
CG = 32
F = 128
H = 640
LEV = 4
NLAT = 64
NLON = 2048


def block_scale(rng, shape, shards, low, top_value):
    gain, own = 1.0, jax.random.fold_in(rng, 6)
    for position, shards_of in shards:
        draws = jnp.exp(jax.random.uniform(jax.random.fold_in(own, position), (shards_of,), jnp.float32, low / len(shards), top_value / len(shards)))
        gain = gain * jnp.repeat(draws, shape[position] // shards_of).reshape([-1 if axis == position else 1 for axis in range(len(shape))])
    return gain


def scatter_about(key, shape, width, reach, pieces=(), kind=jnp.bfloat16):
    level = block_scale(key, shape, pieces, -0.22, 0.18) if pieces else 1.0
    array = jax.random.normal(key, shape, jnp.float32) * width * level
    return jnp.minimum(jnp.maximum(array, -reach), reach).astype(kind)


def setup_inputs(seed: int = 0) -> dict:
    key_of = jax.random.split(jax.random.key(seed), 9)
    latents = scatter_about(key_of[0], (LEV, C, NLAT, NLON), 1.0, 6.0, ((1, 2), (2, 4), (3, 16)))
    conv_weight = scatter_about(key_of[1], (C, 27, C), (27 * C) ** -0.5, 0.15625, ((0, 2),))
    gdn_gamma = jnp.clip(0.1 * jax.random.uniform(key_of[2], (C, CG), jnp.float32) ** block_scale(key_of[2], (C, CG), ((0, 2),), -0.2, 0.2), 0.0, 0.1)
    gdn_beta = jnp.clip(jnp.exp(math.log(2.0) - 1.3862944 * jax.random.uniform(key_of[3], (C,), jnp.float32) ** block_scale(key_of[3], (C,), ((0, 2),), -0.2, 0.2)), 0.5, 2.0)
    hidden_weight = scatter_about(key_of[4], (F, H), F ** -0.5, 0.5)
    hidden_bias = scatter_about(key_of[5], (H,), 0.5, 3.0, (), jnp.float32)
    param_weight = scatter_about(key_of[6], (H, 2 * F), H ** -0.5, 0.25)
    param_bias = scatter_about(key_of[7], (2 * F,), 0.5, 3.0, (), jnp.float32)
    return {"latents": latents, "conv_weight": conv_weight, "gdn_gamma": gdn_gamma, "gdn_beta": gdn_beta, "hidden_weight": hidden_weight, "hidden_bias": hidden_bias, "param_weight": param_weight, "param_bias": param_bias}


highest = lax.Precision.HIGHEST

def entropy_block(features, targets, hidden_weight, hidden_bias, param_weight, param_bias, patch_total):
    pre_act = jnp.dot(features, hidden_weight, preferred_element_type=jnp.float32) + hidden_bias
    hidden = jax.nn.silu(pre_act).astype(jnp.bfloat16)
    params = jnp.dot(hidden, param_weight, preferred_element_type=jnp.float32) + param_bias
    feat_width = features.shape[1]
    centre = params[:, :feat_width]
    raw_spread = params[:, feat_width:]
    spread = 0.5 + jax.nn.softplus(raw_spread)
    scaled_error = (targets.astype(jnp.float32) - centre) / spread
    d_centre = -scaled_error / spread / patch_total
    d_spread = (1.0 - scaled_error * scaled_error) / spread * jax.nn.sigmoid(raw_spread) / patch_total
    d_targets = (scaled_error / spread / patch_total).astype(jnp.bfloat16)
    d_params = jnp.concatenate([d_centre, d_spread], axis=1).astype(jnp.bfloat16)
    grad_pw = jnp.dot(hidden.T, d_params, preferred_element_type=jnp.float32)
    grad_pb = lax.optimization_barrier(jnp.sum(d_params.astype(jnp.float32), axis=0))
    d_hidden = jnp.dot(d_params, param_weight.T, preferred_element_type=jnp.float32)
    sig_gate = jax.nn.sigmoid(pre_act)
    d_pre = (d_hidden * sig_gate * (1.0 + pre_act * (1.0 - sig_gate))).astype(jnp.bfloat16)
    grad_hw = jnp.dot(features.T, d_pre, preferred_element_type=jnp.float32)
    grad_hb = lax.optimization_barrier(jnp.sum(d_pre.astype(jnp.float32), axis=0))
    d_features = jnp.dot(d_pre, hidden_weight.T, preferred_element_type=jnp.float32).astype(jnp.bfloat16)
    return ((grad_hw, grad_hb, grad_pw, grad_pb), d_features, d_targets)

def reference(latents, conv_weight, gdn_gamma, gdn_beta, hidden_weight, hidden_bias, param_weight, param_bias):
    levels, channels, lat_total, lon_total = latents.shape
    group_width = channels // GROUPS
    feat_width = 4 * group_width
    padded = jnp.concatenate([latents[..., -1:], latents, latents[..., :1]], axis=3)
    padded = jnp.pad(padded, ((1, 1), (0, 0), (1, 1), (0, 0))).astype(jnp.float32)
    operand = jnp.transpose(padded, (1, 0, 2, 3))[None]
    kernel = jnp.transpose(conv_weight.astype(jnp.float32).reshape(channels, 3, 3, 3, channels), (0, 4, 1, 2, 3))

    def convolve(kern):
        result = lax.conv_general_dilated(operand, kern, (1, 1, 1), 'VALID', dimension_numbers=('NCDHW', 'OIDHW', 'NCDHW'), precision=highest)
        return jnp.transpose(result[0], (1, 0, 2, 3))
    conv_out, pullback = jax.vjp(convolve, kernel)
    grouped = conv_out.reshape(levels, GROUPS, group_width, lat_total, lon_total)
    gamma_blocks = gdn_gamma.reshape(GROUPS, group_width, group_width)
    denominator = gdn_beta.reshape(GROUPS, group_width)[None, :, :, None, None] + jnp.einsum('goj,lgjab->lgoab', gamma_blocks, grouped * grouped, precision=highest)
    inv_root = lax.rsqrt(denominator)
    normed = (grouped * inv_root).astype(jnp.bfloat16)
    patches = normed.reshape(levels, GROUPS, group_width, lat_total // 2, 2, lon_total // 2, 2)
    patches = jnp.transpose(patches, (1, 0, 3, 5, 4, 6, 2)).reshape(GROUPS, levels, -1, feat_width)
    patch_total = levels * lat_total * lon_total // 4

    def one_block(totals, pair_rows):
        grads, d_features, d_targets = entropy_block(pair_rows[0], pair_rows[1], hidden_weight, hidden_bias, param_weight, param_bias, patch_total)
        return (tuple((left + right for left, right in zip(totals, grads))), (d_features, d_targets))
    initial = (jnp.zeros(hidden_weight.shape, jnp.float32), jnp.zeros(hidden_bias.shape, jnp.float32), jnp.zeros(param_weight.shape, jnp.float32), jnp.zeros(param_bias.shape, jnp.float32))
    totals, back_rows = lax.scan(one_block, initial, (patches[0], patches[1]))
    d_patches = jnp.stack([back_rows[0], back_rows[1]], axis=0)
    d_patches = d_patches.reshape(GROUPS, levels, lat_total // 2, lon_total // 2, 2, 2, group_width)
    d_normed = jnp.transpose(d_patches, (1, 0, 6, 2, 4, 3, 5)).reshape(levels, GROUPS, group_width, lat_total, lon_total).astype(jnp.float32)
    weighted = d_normed * grouped * inv_root / denominator
    d_conv = (d_normed * inv_root - grouped * jnp.einsum('gco,lgcab->lgoab', gamma_blocks, weighted, precision=highest)).astype(jnp.bfloat16)
    kernel_grad = pullback(d_conv.astype(jnp.float32).reshape(levels, channels, lat_total, lon_total))[0]
    conv_grad = jnp.transpose(kernel_grad, (0, 2, 3, 4, 1)).reshape(channels, 27 * channels)
    return (conv_grad, totals[0], totals[1], totals[2], totals[3])
```

```python
import jax
import jax.numpy as jnp
from jax import lax
from jax.experimental import pallas as pl
from jax.experimental.pallas import tpu as pltpu
from jax.sharding import PartitionSpec as P

BF = jnp.bfloat16
F32 = jnp.float32
MESH = pl.DeviceIdType.MESH
PATCHES = 131072.0

NN = (((1,), (0,)), ((), ()))
NT = (((1,), (1,)), ((), ()))


def mm(a, b, dims=NN):
    return lax.dot_general(a, b, dims, preferred_element_type=F32)


def iota(shape, dim):
    return lax.broadcasted_iota(jnp.int32, shape, dim)


def onehot(condition):
    return jnp.where(condition, 1.0, 0.0).astype(BF)


def split(value):
    high = value.astype(BF)
    return high, (value - high.astype(F32)).astype(BF)


class Place:
    def __init__(self):
        self.lon = lax.axis_index("lon")
        self.lat = lax.axis_index("lat")
        self.ch = lax.axis_index("ch")
        self.core = self.lon % 2
        self.y = (self.lon // 2) % 4
        self.zlo = self.lon // 8
        self.x = self.lat
        self.z = self.ch * 2 + self.zlo

    def chip(self, x, y, z, core):
        return ((z % 2) * 8 + y * 2 + core, x, z // 2)

    def sibling(self):
        return self.chip(self.x, self.y, self.z, 1 - self.core)

    def along_x(self, d):
        return self.chip((self.x + d) % 4, self.y, self.z, self.core)

    def along_y(self, d):
        return self.chip(self.x, (self.y + d) % 4, self.z, self.core)

    def along_z(self, d):
        return self.chip(self.x, self.y, (self.z + d) % 4, self.core)

    def along_first(self, d):
        on_x = 1 - self.core
        return self.chip(
            (self.x + d * on_x) % 4, (self.y + d * (1 - on_x)) % 4, self.z, self.core
        )

    def along_second(self, d):
        on_x = self.core
        return self.chip(
            (self.x + d * on_x) % 4, (self.y + d * (1 - on_x)) % 4, self.z, self.core
        )


def remote(src, dst, send, recv, device):
    return pltpu.make_async_remote_copy(
        src_ref=src,
        dst_ref=dst,
        send_sem=send,
        recv_sem=recv,
        device_id=device,
        device_id_type=MESH,
    )


def enter(place):
    lon, lat, ch = place.lon, place.lat, place.ch
    barrier = pltpu.get_barrier_semaphore()
    row = lat + 2 * ch - 1
    row = (row + 4) % 4
    sources = [(lon, lat, 1 - ch), (lon, row, 0), (lon, row, 1)]
    for side in (1, 15):
        for other in (0, 1):
            sources.append(((lon + side) % 16, lat, other))
            sources.append(((lon + side) % 16, row, other))
    sources.append(place.sibling())
    for d in (1, 2, 3):
        sources += [place.along_x(d), place.along_y(d), place.along_z(d)]
    for device in sources:
        pl.semaphore_signal(barrier, inc=1, device_id=device, device_id_type=MESH)
    return barrier, len(sources)


def shuffle_latents(x_ref, own, rim_out):
    rows, cols = iota((512, 512), 0), iota((512, 512), 1)
    swap = onehot(cols == (rows % 32) * 16 + rows // 32)
    b, n = iota((128, 256), 0), iota((128, 256), 1)
    parity = jnp.where(n < 64, 2 * n, 2 * (n - 64) + 1)
    edge = jnp.where(n < 192, 0, 127)
    spread = onehot(b == jnp.where(n < 128, parity, edge))
    r, j = iota((512, 128), 0), iota((512, 128), 1)
    rims = jnp.zeros((512, 128), F32)
    sorted_levels = []
    for level in range(4):
        block = mm(x_ref[level].reshape(512, 128), spread)
        rims = jnp.where((j % 64) == (r % 16) * 4 + level, block[:, 128:], rims)
        sorted_levels.append(block[:, :128].astype(BF))
    for level in range(4):
        own[:, level] = mm(swap, sorted_levels[level]).astype(BF).reshape(16, 32, 128)
    c, k = iota((32, 512), 0), iota((32, 512), 1)
    rim_out[...] = mm(onehot(k // 16 == c), rims.astype(BF)).astype(BF)


def prepare_small(hw_ref, hb_ref, pw_ref, pb_ref, hwt, pwt, hbt, pbt):
    eye = onehot(iota((128, 128), 0) == iota((128, 128), 1))
    for k in range(5):
        part = slice(128 * k, 128 * k + 128)
        hwt[part, :] = mm(eye, hw_ref[:, part], NT).astype(BF)
        hbt[part, :] = jnp.broadcast_to(hb_ref[:, part], (128, 128)).T
    for k in range(2):
        part = slice(128 * k, 128 * k + 128)
        pwt[part, :] = mm(eye, pw_ref[:, part], NT).astype(BF)
        pbt[part, :] = jnp.broadcast_to(pb_ref[:, part], (128, 128)).T


def build_gamma(gall, gam, gamt, beta):
    k, n = iota((128, 256), 0), iota((128, 256), 1)
    copies = onehot(k == n % 32)
    for g in range(2):
        high, low = split(gall[g])
        for which, part in ((0, high), (1, low)):
            wide = mm(part, copies)
            for s in range(4):
                block = g * 4 + s
                own_block = iota((32, 256), 1) // 32 == block
                gam[which, block * 32 : block * 32 + 32, :] = jnp.where(own_block, wide, 0.0)
        for s in range(4):
            block = g * 4 + s
            beta[block * 32 : block * 32 + 32, :] = jnp.broadcast_to(
                gall[g][:, 64:65], (32, 256)
            )
    for which in range(2):
        gamt[which] = gam[which].T


def build_weights(wall, wf):
    lane = iota((32, 256), 1)
    for g in range(2):
        for n in range(9):
            dl, da = n // 3, n % 3
            base = (192 * n) // 128 * 128
            v = wall[g, :, base : base + 256].astype(F32)
            first = v if n % 2 == 0 else pltpu.roll(v, 192, 1)
            second = v if n % 2 == 1 else pltpu.roll(v, 64, 1)
            first = jnp.where(lane < 192, first, 0.0).astype(BF)
            second = jnp.where(lane >= 64, second, 0.0).astype(BF)
            for p in range(2):
                r = da + p
                row = g * 128 + 2 * p * 32
                wf[dl, row : row + 32, 256 * r : 256 * r + 256] = first
                wf[dl, row + 32 : row + 64, 256 * r : 256 * r + 256] = second
        for dl in range(3):
            for p in range(2):
                r = 3 if p == 0 else 0
                row = g * 128 + 2 * p * 32
                wf[dl, row : row + 64, 256 * r : 256 * r + 256] = jnp.zeros((64, 256), BF)


def build_windows(place, field, rim_in, rims, xt):
    chi, lat = place.ch, place.lat
    k, n = iota((512, 128), 0), iota((512, 128), 1)
    block, kk, nn = k // 128, k % 128, n % 64
    left = block < 2
    same = block % 2 == 0
    pole = jnp.where(chi == 0, lat, 3 - lat) == 0
    shift_same = (8 * chi - 1) * 4
    other_low = 36 * chi
    shift_other = jnp.where(chi == 0, 60, -36)
    shift = jnp.where(same, shift_same, shift_other)
    source = nn + shift
    inside = (source >= 0) & (source < 64) & (nn < 40)
    only = (nn >= other_low) & (nn < other_low + 4) & jnp.logical_not(pole)
    valid = inside & (same | only)
    side = (left & (n < 64)) | (jnp.logical_not(left) & (n >= 64))
    chosen = kk == source + jnp.where(left, 64, 0)
    pick = onehot(valid & side & chosen)
    tiles = jnp.concatenate(
        [rim_in[s, t].reshape(64, 128) for s in range(2) for t in range(2)], axis=1
    )
    rims[...] = mm(tiles, pick)

    col = iota((1, 512), 1)
    w, js, m = col // 128, (col % 128) // 64, col % 64
    target = jnp.where(
        w == 0,
        jnp.where(m == 0, 256 + js * 8, js * 128 + 63 + m),
        jnp.where(
            w == 1,
            js * 128 + m,
            jnp.where(
                w == 2,
                js * 128 + 64 + m,
                jnp.where(m == 63, 320 + js * 8, js * 128 + m + 1),
            ),
        ),
    )
    pick2 = onehot(iota((384, 512), 0) == target)
    for r in range(4):
        for pair in range(2):
            j0 = r + 4 * pair
            j1 = j0 + 2
            stack = []
            for level in range(4):
                edge = pltpu.roll(rims[...], 128 - (j0 * 4 + level), 1).astype(BF)
                stack.append(
                    jnp.concatenate(
                        [
                            field[j0, level].reshape(64, 128),
                            field[j1, level].reshape(64, 128),
                            edge,
                        ],
                        axis=1,
                    )
                )
            out = mm(jnp.concatenate(stack, axis=0), pick2).astype(BF)
            for level in range(4):
                for v in range(4):
                    lane = level * 256 + pair * 128
                    xt[r * 256 + v * 64 : r * 256 + v * 64 + 64, lane : lane + 128] = out[
                        level * 64 : level * 64 + 64, v * 128 : v * 128 + 128
                    ]


def mix(gam, value):
    high, low = split(value)
    ghigh, glow = gam[0].astype(BF), gam[1].astype(BF)
    return mm(ghigh, high) + (mm(ghigh, low) + mm(glow, high))


def forward(s):
    for level in range(4):
        lanes = slice(256 * level, 256 * level + 256)
        total = None
        for dl in range(3):
            other = level + dl - 1
            if 0 <= other < 4:
                term = mm(s["wf"][dl], s["xt"][:, 256 * other : 256 * other + 256])
                total = term if total is None else total + term
        s["conv"][:, lanes] = total
    for level in range(4):
        lanes = slice(256 * level, 256 * level + 256)
        total = s["conv"][:, lanes]
        inv = lax.rsqrt(s["beta"][...] + mix(s["gam"], total * total))
        s["inv"][:, lanes] = inv
        s["normed"][:, lanes] = (total * inv).astype(BF)


def entropy(s, hw_ref, pw_ref):
    def first(i, carry):
        lanes = pl.ds(pl.multiple_of(i * 256, 256), 256)
        features = s["normed"][0:128, lanes]
        for k in range(5):
            part = slice(128 * k, 128 * k + 128)
            bias = s["hbt"][part, :]
            pre = mm(s["hwt"][part, :], features) + jnp.concatenate([bias, bias], axis=1)
            sig = 1.0 / (1.0 + jnp.exp(-pre))
            act = pre * sig
            s["hidden"][part, lanes] = act.astype(BF)
            s["gate"][part, lanes] = sig * (1.0 + pre - act)
        return carry

    lax.fori_loop(0, 4, first, 0)

    def second(i, carry):
        lanes = pl.ds(pl.multiple_of(i * 256, 256), 256)
        hidden = s["hidden"][:, lanes]
        cb, rb = s["pbt"][0:128, :], s["pbt"][128:256, :]
        centre = mm(s["pwt"][0:128, :], hidden) + jnp.concatenate([cb, cb], axis=1)
        raw = mm(s["pwt"][128:256, :], hidden) + jnp.concatenate([rb, rb], axis=1)
        small = jnp.exp(-jnp.abs(raw))
        spread = 0.5 + jnp.maximum(raw, 0.0) + jnp.log1p(small)
        sig = jnp.where(raw >= 0.0, 1.0, small) / (1.0 + small)
        over = 1.0 / spread
        error = (s["normed"][128:256, lanes].astype(F32) - centre) * over
        ratio = error * over * (1.0 / PATCHES)
        s["dparams"][0:128, lanes] = (-ratio).astype(BF)
        s["dparams"][128:256, lanes] = (
            (1.0 - error * error) * over * sig * (1.0 / PATCHES)
        ).astype(BF)
        s["dtargets"][:, lanes] = ratio.astype(BF)
        return carry

    lax.fori_loop(0, 4, second, 0)

    ones = jnp.ones((8, 1024), BF)
    grad = mm(s["hidden"][...], s["dparams"][...], NT)
    part = s["part"]
    for half in range(2):
        block = grad[:, 128 * half : 128 * half + 128]
        part[40 * half : 40 * half + 40] = block.reshape(40, 16, 128)
    pb = mm(ones, s["dparams"][...], NT)

    def third(i, carry):
        lanes = pl.ds(pl.multiple_of(i * 256, 256), 256)
        back = mm(pw_ref[...], s["dparams"][:, lanes])
        s["dpre"][:, lanes] = (back * s["gate"][:, lanes]).astype(BF)
        return carry

    lax.fori_loop(0, 4, third, 0)
    grad = mm(s["normed"][0:128, :], s["dpre"][...], NT)
    for k in range(5):
        block = grad[:, 128 * k : 128 * k + 128]
        part[80 + 8 * k : 88 + 8 * k] = block.reshape(8, 16, 128)
    hb = mm(ones, s["dpre"][...], NT)
    zeros = jnp.zeros((1, 128), F32)
    lines = [hb[0:1, 128 * k : 128 * k + 128] for k in range(5)]
    lines += [pb[0:1, 0:128], pb[0:1, 128:256]] + [zeros] * 9
    part[120] = jnp.concatenate(lines, axis=0)
    part[121:128] = jnp.zeros((7, 16, 128), F32)


def backward(s, hw_ref):
    for level in range(4):
        lanes = slice(256 * level, 256 * level + 256)
        dfeat = mm(hw_ref[...], s["dpre"][:, lanes]).astype(BF).astype(F32)
        dn = jnp.concatenate([dfeat, s["dtargets"][:, lanes].astype(F32)], axis=0)
        inv = s["inv"][:, lanes]
        y = s["conv"][:, lanes]
        dni = dn * inv
        weighted = dni * y * (inv * inv)
        s["dconv"][:, lanes] = (dni - y * mix(s["gamt"], weighted)).astype(BF)
    for dl in range(3):
        first, last = max(0, 1 - dl), min(4, 5 - dl)
        d = s["dconv"][:, 256 * first : 256 * last]
        x = s["xt"][:, 256 * (first + dl - 1) : 256 * (last + dl - 1)]
        s["taps"][dl] = mm(d, x, NT)
    for dl in range(3):
        for da in range(3):
            n = dl * 3 + da
            for g in range(2):
                total = None
                for p in range(2):
                    row = g * 128 + 2 * p * 32
                    lanes = slice(256 * (da + p), 256 * (da + p) + 256)
                    a = s["taps"][dl, row : row + 32, lanes]
                    b = s["taps"][dl, row + 32 : row + 64, lanes]
                    term = a + pltpu.roll(b, 192, 1)
                    total = term if total is None else total + term
                s["wgrad"][32 * g : 32 * g + 32, 192 * n : 192 * n + 192] = total[:, 0:192]
    s["wgrad"][:, 1728:2048] = jnp.zeros((64, 320), F32)
    for k in range(16):
        start = 108 * k
        base = start // 128 * 128
        shift = (256 - (start - base)) % 256
        v = s["wgrad"][:, base : base + 256]
        v = pltpu.roll(v, shift, 1)[:, 0:128] if shift else v[:, 0:128]
        core, y, zlo = k % 2, (k // 2) % 4, k // 8
        for g in range(2):
            s["cpart"][core, g * 2 + zlo, y] = v[32 * g : 32 * g + 32, :]


def body(
    x_ref, wl_ref, gb_ref, hw_ref, hb_ref, pw_ref, pb_ref,
    cg_ref, hwg_ref, hbg_ref, pwg_ref, pbg_ref,
    own, rim_out, rim_in, field, wall, gall, rims,
    xt, wf, gam, gamt, beta, hwt, pwt, hbt, pbt,
    conv, inv, normed, hidden, gate, dparams, dtargets, dpre, dconv, taps, wgrad,
    part, cpart, total, r1, r2, r3, r4, q1, q2, q3, q4,
    local_sem, xs, xr, as_, ar, cs, cr,
):
    place = Place()
    lon, lat, chi = place.lon, place.lat, place.ch
    partner = (lon, lat, 1 - chi)
    barrier, count = enter(place)

    locals_ = [
        pltpu.make_async_copy(wl_ref, wall.at[chi], local_sem.at[0]),
        pltpu.make_async_copy(gb_ref, gall.at[chi], local_sem.at[1]),
    ]
    for copy in locals_:
        copy.start()
    shuffle_latents(x_ref, own, rim_out)
    pl.semaphore_wait(barrier, count)

    sends = []
    sends.append(
        remote(
            own.at[pl.ds(7 * (1 - chi), 9)],
            field.at[pl.ds(chi, 9), :, chi],
            xs.at[0], xr.at[0], partner,
        )
    )
    sends.append(remote(wl_ref, wall.at[chi], xs.at[1], xr.at[1], partner))
    sends.append(remote(gb_ref, gall.at[chi], xs.at[2], xr.at[2], partner))
    down, up = (lat + 3) % 4, (lat + 1) % 4
    sends.append(
        remote(own.at[0], field.at[9, :, chi], xs.at[3], xr.at[3 + chi], (lon, down, 1))
    )
    sends.append(
        remote(own.at[15], field.at[0, :, chi], xs.at[4], xr.at[3 + chi], (lon, up, 0))
    )
    for side in range(2):
        near = (lon + 1) % 16 if side == 0 else (lon + 15) % 16
        for kind, (row, half) in enumerate(((lat, 0), (lat, 1), (down, 1), (up, 0))):
            other = kind // 2
            slot = 5 + (side * 2 + other) * 2
            sends.append(
                remote(
                    rim_out,
                    rim_in.at[side, other, chi],
                    xs.at[5 + side * 4 + kind], xr.at[slot + chi], (near, row, half),
                )
            )
    for copy in sends:
        copy.start()
    mine = pltpu.make_async_copy(
        own.at[pl.ds(7 * chi, 9)], field.at[pl.ds(1 - chi, 9), :, chi], local_sem.at[2]
    )
    mine.start()
    prepare_small(hw_ref, hb_ref, pw_ref, pb_ref, hwt, pwt, hbt, pbt)
    for copy in locals_:
        copy.wait()
    mine.wait()
    other = 1 - chi
    remote(gb_ref, gall.at[other], xs.at[2], xr.at[2], partner).wait_recv()
    build_gamma(gall, gam, gamt, beta)
    remote(wl_ref, wall.at[other], xs.at[1], xr.at[1], partner).wait_recv()
    build_weights(wall, wf)
    for half in range(2):
        remote(
            own.at[0], field.at[9 * chi, :, half], xs.at[3], xr.at[3 + half], partner
        ).wait_recv()
    for side in range(2):
        for kind in range(2):
            for half in range(2):
                remote(
                    rim_out, rim_in.at[side, kind, half], xs.at[5],
                    xr.at[5 + (side * 2 + kind) * 2 + half], partner,
                ).wait_recv()
    remote(
        own.at[pl.ds(0, 9)], field.at[pl.ds(1 - chi, 9), :, other], xs.at[0], xr.at[0], partner
    ).wait_recv()

    @pl.when(jnp.where(chi == 0, lat, 3 - lat) == 0)
    def _():
        field[9 * chi] = jnp.zeros(field.shape[1:], BF)

    build_windows(place, field, rim_in, rims, xt)
    s = {
        "xt": xt, "wf": wf, "gam": gam, "gamt": gamt, "beta": beta, "hwt": hwt, "pwt": pwt,
        "hbt": hbt, "pbt": pbt, "conv": conv, "inv": inv, "normed": normed, "hidden": hidden,
        "gate": gate, "dparams": dparams, "dtargets": dtargets, "dpre": dpre, "dconv": dconv,
        "taps": taps, "wgrad": wgrad, "part": part, "cpart": cpart,
    }
    forward(s)
    entropy(s, hw_ref, pw_ref)
    backward(s, hw_ref)

    core, x, y, z = place.core, place.x, place.y, place.z
    c1 = jnp.where(core == 0, x, y)
    c2 = jnp.where(core == 0, y, x)
    sibling = place.sibling()

    def pair_of(d):
        return (4 - d) % 4

    at = lambda ref, *index: ref.at[index]
    groups = part.reshape(2, 4, 4, 4, 16, 128)
    totals = total.reshape(2, 4, 4, 4, 16, 128)

    def go(copies):
        for copy in copies:
            copy.start()
        sends.extend(copies)
        for copy in copies:
            copy.wait_recv()

    go([
        remote(groups.at[1 - core], r1, as_.at[0], ar.at[0], sibling),
        remote(cpart.at[1 - core], q1, cs.at[0], cr.at[0], sibling),
    ])
    groups[core] = groups[core] + r1[...]
    cpart[core] = cpart[core] + q1[...]
    go(
        [
            remote(
                groups.at[core, (c1 + d) % 4], r2.at[d - 1], as_.at[d], ar.at[d],
                place.along_first(d),
            )
            for d in (1, 2, 3)
        ]
        + [
            remote(
                cpart.at[core, (z + d) % 4], q2.at[d - 1], cs.at[d], cr.at[d], place.along_z(d)
            )
            for d in (1, 2, 3)
        ]
    )
    groups[core, c1] = (groups[core, c1] + r2[0]) + (r2[1] + r2[2])
    cpart[core, z] = (cpart[core, z] + q2[0]) + (q2[1] + q2[2])
    go(
        [
            remote(
                groups.at[core, c1, (c2 + d) % 4], r3.at[d - 1], as_.at[3 + d], ar.at[3 + d],
                place.along_second(d),
            )
            for d in (1, 2, 3)
        ]
        + [
            remote(
                cpart.at[core, z, (y + d) % 4], q3.at[d - 1], cs.at[3 + d], cr.at[3 + d],
                place.along_y(d),
            )
            for d in (1, 2, 3)
        ]
    )
    groups[core, c1, c2] = (groups[core, c1, c2] + r3[0]) + (r3[1] + r3[2])
    cpart[core, z, y] = (cpart[core, z, y] + q3[0]) + (q3[1] + q3[2])
    go(
        [
            remote(
                groups.at[core, c1, c2, (z + d) % 4], r4.at[d - 1], as_.at[6 + d], ar.at[6 + d],
                place.along_z(d),
            )
            for d in (1, 2, 3)
        ]
        + [
            remote(
                cpart.at[core, z, y], q4.at[d - 1], cs.at[6 + d], cr.at[6 + d], place.along_x(d)
            )
            for d in (1, 2, 3)
        ]
    )
    totals[core, c1, c2, z] = (groups[core, c1, c2, z] + r4[0]) + (r4[1] + r4[2])
    block = (cpart[core, z, y] + q4[0]) + (q4[1] + q4[2])
    cg_ref[...] = pltpu.roll(block, (128 - 27 * x) % 128, 1)[:, 0:27]

    def gather(view, stage, along, received):
        copies = [
            remote(view, view, as_.at[stage + d], ar.at[stage + d], along(d)) for d in (1, 2, 3)
        ]
        for copy in copies:
            copy.start()
        sends.extend(copies)
        for d in (1, 2, 3):
            remote(
                view, received((4 - d) % 4), as_.at[stage + d], ar.at[stage + d], along(d)
            ).wait_recv()

    gather(
        totals.at[core, c1, c2, z], 9, place.along_z, lambda d: totals.at[core, c1, c2, (z + d) % 4]
    )
    gather(totals.at[core, c1, c2], 12, place.along_second, lambda d: totals.at[core, c1, (c2 + d) % 4])
    gather(totals.at[core, c1], 15, place.along_first, lambda d: totals.at[core, (c1 + d) % 4])
    last = remote(totals.at[core], totals.at[core], as_.at[19], ar.at[19], sibling)
    last.start()
    sends.append(last)
    remote(
        totals.at[core], totals.at[1 - core], as_.at[19], ar.at[19], sibling
    ).wait_recv()

    for half in range(2):
        pwg_ref[:, 128 * half : 128 * half + 128] = total[40 * half : 40 * half + 40].reshape(
            640, 128
        )
    for k in range(5):
        hwg_ref[:, 128 * k : 128 * k + 128] = total[80 + 8 * k : 88 + 8 * k].reshape(128, 128)
        hbg_ref[:, 128 * k : 128 * k + 128] = total[120, k : k + 1, :]
    for k in range(2):
        pbg_ref[:, 128 * k : 128 * k + 128] = total[120, 5 + k : 6 + k, :]
    for copy in sends:
        copy.wait_send()


def on_device(x, cw, gamma, beta, hw, hb, pw, pb):
    wl = jnp.pad(cw.reshape(32, 1728), ((0, 0), (0, 64)))
    gb = jnp.concatenate(
        [gamma, jnp.zeros((32, 32), F32), jnp.broadcast_to(beta[:, None], (32, 64))], axis=1
    )
    vmem = pltpu.VMEM
    scratch = [
        vmem((16, 4, 32, 128), BF),
        vmem((32, 128), BF),
        vmem((2, 2, 2, 32, 128), BF),
        vmem((10, 4, 2, 32, 128), BF),
        vmem((2, 32, 1792), BF),
        vmem((2, 32, 128), F32),
        vmem((64, 128), F32),
        vmem((1024, 1024), BF),
        vmem((3, 256, 1024), BF),
        vmem((2, 256, 256), F32),
        vmem((2, 256, 256), F32),
        vmem((256, 256), F32),
        vmem((640, 128), BF),
        vmem((256, 640), BF),
        vmem((640, 128), F32),
        vmem((256, 128), F32),
        vmem((256, 1024), F32),
        vmem((256, 1024), F32),
        vmem((256, 1024), BF),
        vmem((640, 1024), BF),
        vmem((640, 1024), F32),
        vmem((256, 1024), BF),
        vmem((128, 1024), BF),
        vmem((640, 1024), BF),
        vmem((256, 1024), BF),
        vmem((3, 256, 1024), F32),
        vmem((64, 2048), F32),
        vmem((128, 16, 128), F32),
        vmem((2, 4, 4, 32, 128), F32),
        vmem((128, 16, 128), F32),
        vmem((4, 4, 4, 16, 128), F32),
        vmem((3, 4, 4, 16, 128), F32),
        vmem((3, 4, 16, 128), F32),
        vmem((3, 16, 128), F32),
        vmem((4, 4, 32, 128), F32),
        vmem((3, 4, 32, 128), F32),
        vmem((3, 32, 128), F32),
        vmem((3, 32, 128), F32),
        pltpu.SemaphoreType.DMA((3,)),
        pltpu.SemaphoreType.DMA((13,)),
        pltpu.SemaphoreType.DMA((13,)),
        pltpu.SemaphoreType.DMA((20,)),
        pltpu.SemaphoreType.DMA((20,)),
        pltpu.SemaphoreType.DMA((10,)),
        pltpu.SemaphoreType.DMA((10,)),
    ]
    spec = pl.BlockSpec(memory_space=pltpu.VMEM)
    cg, hwg, hbg, pwg, pbg = pl.pallas_call(
        body,
        out_shape=(
            jax.ShapeDtypeStruct((32, 27), F32),
            jax.ShapeDtypeStruct((128, 640), F32),
            jax.ShapeDtypeStruct((1, 640), F32),
            jax.ShapeDtypeStruct((640, 256), F32),
            jax.ShapeDtypeStruct((1, 256), F32),
        ),
        in_specs=[spec] * 7,
        out_specs=(spec,) * 5,
        scratch_shapes=scratch,
        compiler_params=pltpu.CompilerParams(
            collective_id=0, has_side_effects=True, vmem_limit_bytes=56 * 1024 * 1024
        ),
    )(x, wl, gb, hw, hb.reshape(1, 640), pw, pb.reshape(1, 256))
    return cg, hwg, hbg.reshape(640), pwg, pbg.reshape(256)


def solution(mesh):
    placed = (
        P(None, "ch", "lat", "lon"),
        P("ch", None, None),
        P("ch", None),
        P("ch"),
        P(),
        P(),
        P(),
        P(),
    )
    return jax.shard_map(
        on_device,
        mesh=mesh,
        in_specs=placed,
        out_specs=(P("ch", ("lon", "lat")), P(), P(), P(), P()),
        check_vma=False,
    )
```

```python
import jax
import jax.numpy as jnp
from jax import lax
from jax.experimental import pallas as pl
from jax.experimental.pallas import tpu as pltpu
from jax.sharding import PartitionSpec as P

BF = jnp.bfloat16
F32 = jnp.float32
MESH = pl.DeviceIdType.MESH
PATCHES = 131072.0

NN = (((1,), (0,)), ((), ()))
NT = (((1,), (1,)), ((), ()))


def mm(a, b, dims=NN):
    return lax.dot_general(a, b, dims, preferred_element_type=F32)


def iota(shape, dim):
    return lax.broadcasted_iota(jnp.int32, shape, dim)


def onehot(condition):
    return jnp.where(condition, 1.0, 0.0).astype(BF)


def split(value):
    high = value.astype(BF)
    return high, (value - high.astype(F32)).astype(BF)


class Place:
    def __init__(self):
        self.lon = lax.axis_index("lon")
        self.lat = lax.axis_index("lat")
        self.ch = lax.axis_index("ch")
        self.core = self.lon % 2
        self.y = (self.lon // 2) % 4
        self.zlo = self.lon // 8
        self.x = self.lat
        self.z = self.ch * 2 + self.zlo
        self.c1 = jnp.where(self.core == 0, self.x, self.y)
        self.c2 = jnp.where(self.core == 0, self.y, self.x)

    def chip(self, x, y, z, core):
        return ((z % 2) * 8 + y * 2 + core, x, z // 2)

    def sibling(self):
        return self.chip(self.x, self.y, self.z, 1 - self.core)

    def along_x(self, d):
        return self.chip((self.x + d) % 4, self.y, self.z, self.core)

    def along_y(self, d):
        return self.chip(self.x, (self.y + d) % 4, self.z, self.core)

    def along_z(self, d):
        return self.chip(self.x, self.y, (self.z + d) % 4, self.core)

    def along_first(self, d):
        on_x = 1 - self.core
        return self.chip(
            (self.x + d * on_x) % 4, (self.y + d * (1 - on_x)) % 4, self.z, self.core
        )

    def in_plane(self, c2, z):
        x = jnp.where(self.core == 0, self.x, c2)
        y = jnp.where(self.core == 0, c2, self.y)
        return self.chip(x, y, z, self.core)


def remote(src, dst, send, recv, device):
    return pltpu.make_async_remote_copy(
        src_ref=src,
        dst_ref=dst,
        send_sem=send,
        recv_sem=recv,
        device_id=device,
        device_id_type=MESH,
    )


def enter(place):
    lon, lat, ch = place.lon, place.lat, place.ch
    barrier = pltpu.get_barrier_semaphore()
    row = (lat + 2 * ch + 3) % 4
    devices = [(lon, lat, 1 - ch), (lon, row, 0), (lon, row, 1)]
    for side in (1, 15):
        for other in (0, 1):
            devices.append(((lon + side) % 16, lat, other))
            devices.append(((lon + side) % 16, row, other))
    devices.append(place.sibling())
    for d in (1, 2, 3):
        devices += [place.along_x(d), place.along_y(d), place.along_z(d)]
    for a in range(1, 4):
        for d in range(1, 4):
            devices.append(place.in_plane((place.c2 + a) % 4, (place.z + d) % 4))
    for device in devices:
        pl.semaphore_signal(barrier, inc=1, device_id=device, device_id_type=MESH)
    return barrier, len(devices)


def shuffle_latents(x_ref, own, rim_out):
    rows, cols = iota((512, 512), 0), iota((512, 512), 1)
    swap = onehot(cols == (rows % 32) * 16 + rows // 32)
    b, n = iota((128, 256), 0), iota((128, 256), 1)
    parity = jnp.where(n < 64, 2 * n, 2 * (n - 64) + 1)
    edge = jnp.where(n < 192, 0, 127)
    spread = onehot(b == jnp.where(n < 128, parity, edge))
    r, j = iota((512, 128), 0), iota((512, 128), 1)
    rims = jnp.zeros((512, 128), F32)
    for level in range(4):
        block = mm(x_ref[level].reshape(512, 128), spread)
        rims = jnp.where((j % 64) == (r % 16) * 4 + level, block[:, 128:], rims)
        own[level] = mm(swap, block[:, :128].astype(BF)).astype(BF).reshape(16, 32, 128)
    c, k = iota((32, 512), 0), iota((32, 512), 1)
    rim_out[...] = mm(onehot(k // 16 == c), rims.astype(BF)).astype(BF)


def pack_weights(cw_ref, gamma_ref, beta_ref, wl, gb):
    for k in range(13):
        wl[:, 128 * k : 128 * k + 128] = jnp.concatenate(
            [cw_ref[2 * k].astype(F32), cw_ref[2 * k + 1].astype(F32)], axis=1
        ).astype(BF)
    wl[:, 1664:1792] = jnp.concatenate(
        [cw_ref[26].astype(F32), jnp.zeros((32, 64), F32)], axis=1
    ).astype(BF)
    line = beta_ref[...].reshape(1, 32)
    column = jnp.sum(
        jnp.where(iota((32, 32), 0) == iota((32, 32), 1), line, 0.0), axis=1, keepdims=True
    )
    gb[:, 0:32] = gamma_ref[...]
    gb[:, 32:128] = jnp.broadcast_to(column, (32, 96))


def prepare_small(hw, hb_ref, pw, pb_ref, hwt, pwt, hbt, pbt):
    eye = onehot(iota((128, 128), 0) == iota((128, 128), 1))
    for k in range(5):
        part = slice(128 * k, 128 * k + 128)
        hwt[part, :] = mm(eye, hw[:, part], NT).astype(BF)
        hbt[part, :] = jnp.broadcast_to(hb_ref[part].reshape(1, 128), (128, 128)).T
    for k in range(2):
        part = slice(128 * k, 128 * k + 128)
        pwt[part, :] = mm(eye, pw[:, part], NT).astype(BF)
        pbt[part, :] = jnp.broadcast_to(pb_ref[part].reshape(1, 128), (128, 128)).T


def build_gamma(gall, gam, gamt, beta):
    k, n = iota((128, 256), 0), iota((128, 256), 1)
    copies = onehot(k == n % 32)
    for g in range(2):
        high, low = split(gall[g])
        for which, part in ((0, high), (1, low)):
            wide = mm(part, copies)
            for s in range(4):
                block = g * 4 + s
                own_block = iota((32, 256), 1) // 32 == block
                gam[which, block * 32 : block * 32 + 32, :] = jnp.where(own_block, wide, 0.0)
        for s in range(4):
            block = g * 4 + s
            beta[block * 32 : block * 32 + 32, :] = jnp.broadcast_to(
                gall[g][:, 64:65], (32, 256)
            )
    for which in range(2):
        gamt[which] = gam[which].T


def build_weights(wall, wf):
    lane = iota((32, 256), 1)
    for g in range(2):
        for n in range(9):
            dl, da = n // 3, n % 3
            base = (192 * n) // 128 * 128
            v = wall[g, :, base : base + 256].astype(F32)
            first = v if n % 2 == 0 else pltpu.roll(v, 192, 1)
            second = v if n % 2 == 1 else pltpu.roll(v, 64, 1)
            first = jnp.where(lane < 192, first, 0.0).astype(BF)
            second = jnp.where(lane >= 64, second, 0.0).astype(BF)
            for p in range(2):
                r = da + p
                row = g * 128 + 2 * p * 32
                wf[dl, row : row + 32, 256 * r : 256 * r + 256] = first
                wf[dl, row + 32 : row + 64, 256 * r : 256 * r + 256] = second
        for dl in range(3):
            for p in range(2):
                r = 3 if p == 0 else 0
                row = g * 128 + 2 * p * 32
                wf[dl, row : row + 64, 256 * r : 256 * r + 256] = jnp.zeros((64, 256), BF)


def place_rims(place, rim_in, rims):
    chi, lat = place.ch, place.lat
    k, n = iota((512, 128), 0), iota((512, 128), 1)
    block, kk, nn = k // 128, k % 128, n % 64
    left = block < 2
    same = block % 2 == 0
    pole = jnp.where(chi == 0, lat, 3 - lat) == 0
    shift_same = (8 * chi - 1) * 4
    other_low = 36 * chi
    shift_other = jnp.where(chi == 0, 60, -36)
    shift = jnp.where(same, shift_same, shift_other)
    source = nn + shift
    inside = (source >= 0) & (source < 64) & (nn < 40)
    only = (nn >= other_low) & (nn < other_low + 4) & jnp.logical_not(pole)
    valid = inside & (same | only)
    side = (left & (n < 64)) | (jnp.logical_not(left) & (n >= 64))
    chosen = kk == source + jnp.where(left, 64, 0)
    pick = onehot(valid & side & chosen)
    tiles = jnp.concatenate(
        [rim_in[s, t].reshape(64, 128) for s in range(2) for t in range(2)], axis=1
    )
    rims[...] = mm(tiles, pick)


def window_pick():
    col = iota((1, 512), 1)
    w, js, m = col // 128, (col % 128) // 64, col % 64
    target = jnp.where(
        w == 0,
        jnp.where(m == 0, 256 + js * 8, js * 128 + 63 + m),
        jnp.where(
            w == 1,
            js * 128 + m,
            jnp.where(
                w == 2,
                js * 128 + 64 + m,
                jnp.where(m == 63, 320 + js * 8, js * 128 + m + 1),
            ),
        ),
    )
    return onehot(iota((384, 512), 0) == target)


def build_windows(field, rims, pick, xt, level):
    stack = []
    for r in range(4):
        for pair in range(2):
            j0 = r + 4 * pair
            edge = pltpu.roll(rims[...], 128 - (j0 * 4 + level), 1).astype(BF)
            rows = [field[level, :, j].reshape(64, 128) for j in (j0, j0 + 2)]
            stack.append(jnp.concatenate(rows + [edge], axis=1))
    out = mm(jnp.concatenate(stack, axis=0), pick[...]).astype(BF)
    for r in range(4):
        for pair in range(2):
            row, lane = (r * 2 + pair) * 64, level * 256 + pair * 128
            for v in range(4):
                xt[r * 256 + v * 64 : r * 256 + v * 64 + 64, lane : lane + 128] = out[
                    row : row + 64, v * 128 : v * 128 + 128
                ]


def mix(gam, value):
    high, low = split(value)
    ghigh, glow = gam[0].astype(BF), gam[1].astype(BF)
    return mm(ghigh, high) + (mm(ghigh, low) + mm(glow, high))


def forward(s, level):
    lanes = slice(256 * level, 256 * level + 256)
    total = None
    for dl in range(3):
        other = level + dl - 1
        if 0 <= other < 4:
            term = mm(s["wf"][dl], s["xt"][:, 256 * other : 256 * other + 256])
            total = term if total is None else total + term
    s["conv"][:, lanes] = total
    inv = lax.rsqrt(s["beta"][...] + mix(s["gam"], total * total))
    s["inv"][:, lanes] = inv
    s["normed"][:, lanes] = (total * inv).astype(BF)


def entropy_forward(s):
    def first(i, carry):
        lanes = pl.ds(pl.multiple_of(i * 256, 256), 256)
        features = s["normed"][0:128, lanes]
        for k in range(5):
            part = slice(128 * k, 128 * k + 128)
            bias = s["hbt"][part, :]
            pre = mm(s["hwt"][part, :], features) + jnp.concatenate([bias, bias], axis=1)
            sig = 1.0 / (1.0 + jnp.exp(-pre))
            act = pre * sig
            s["hidden"][part, lanes] = act.astype(BF)
            s["gate"][part, lanes] = sig * (1.0 + pre - act)
        return carry

    lax.fori_loop(0, 4, first, 0)

    def second(i, carry):
        lanes = pl.ds(pl.multiple_of(i * 256, 256), 256)
        hidden = s["hidden"][:, lanes]
        cb, rb = s["pbt"][0:128, :], s["pbt"][128:256, :]
        centre = mm(s["pwt"][0:128, :], hidden) + jnp.concatenate([cb, cb], axis=1)
        raw = mm(s["pwt"][128:256, :], hidden) + jnp.concatenate([rb, rb], axis=1)
        small = jnp.exp(-jnp.abs(raw))
        spread = 0.5 + jnp.maximum(raw, 0.0) + jnp.log1p(small)
        sig = jnp.where(raw >= 0.0, 1.0, small) / (1.0 + small)
        over = 1.0 / spread
        error = (s["normed"][128:256, lanes].astype(F32) - centre) * over
        ratio = error * over * (1.0 / PATCHES)
        s["dparams"][0:128, lanes] = (-ratio).astype(BF)
        s["dparams"][128:256, lanes] = (
            (1.0 - error * error) * over * sig * (1.0 / PATCHES)
        ).astype(BF)
        s["dtargets"][:, lanes] = ratio.astype(BF)
        return carry

    lax.fori_loop(0, 4, second, 0)

    grad = mm(s["hidden"][...], s["dparams"][...], NT)
    for half in range(2):
        for k in range(4):
            s["part"][half, k, 0:10] = grad[
                160 * k : 160 * k + 160, 128 * half : 128 * half + 128
            ].reshape(10, 16, 128)


def entropy_backward(s, pw):
    def third(i, carry):
        lanes = pl.ds(pl.multiple_of(i * 256, 256), 256)
        back = mm(pw[...], s["dparams"][:, lanes])
        s["dpre"][:, lanes] = (back * s["gate"][:, lanes]).astype(BF)
        return carry

    lax.fori_loop(0, 4, third, 0)


def hidden_grads(s):
    part = s["part"]
    ones = jnp.ones((8, 1024), BF)
    pb = mm(ones, s["dparams"][...], NT)
    grad = mm(s["normed"][0:128, :], s["dpre"][...], NT)
    for k in range(5):
        for n in range(8):
            part[n // 4, n % 4, 10 + k] = grad[16 * n : 16 * n + 16, 128 * k : 128 * k + 128]
    hb = mm(ones, s["dpre"][...], NT)
    zeros = jnp.zeros((1, 128), F32)
    lines = [hb[0:1, 128 * k : 128 * k + 128] for k in range(5)]
    lines += [pb[0:1, 0:128], pb[0:1, 128:256]] + [zeros] * 9
    for n in range(8):
        part[n // 4, n % 4, 15] = jnp.zeros((16, 128), F32)
    part[0, 0, 15] = jnp.concatenate(lines, axis=0)


def conv_backward(s, hw):
    for level in range(4):
        lanes = slice(256 * level, 256 * level + 256)
        dfeat = mm(hw[...], s["dpre"][:, lanes]).astype(BF).astype(F32)
        dn = jnp.concatenate([dfeat, s["dtargets"][:, lanes].astype(F32)], axis=0)
        inv = s["inv"][:, lanes]
        y = s["conv"][:, lanes]
        dni = dn * inv
        weighted = dni * y * (inv * inv)
        s["dconv"][:, lanes] = (dni - y * mix(s["gamt"], weighted)).astype(BF)


def weight_grads(s):
    for dl in range(3):
        first, last = max(0, 1 - dl), min(4, 5 - dl)
        d = s["dconv"][:, 256 * first : 256 * last]
        x = s["xt"][:, 256 * (first + dl - 1) : 256 * (last + dl - 1)]
        s["taps"][dl] = mm(d, x, NT)
    for dl in range(3):
        for da in range(3):
            n = dl * 3 + da
            for g in range(2):
                total = None
                for p in range(2):
                    row = g * 128 + 2 * p * 32
                    lanes = slice(256 * (da + p), 256 * (da + p) + 256)
                    a = s["taps"][dl, row : row + 32, lanes]
                    b = s["taps"][dl, row + 32 : row + 64, lanes]
                    term = a + pltpu.roll(b, 192, 1)
                    total = term if total is None else total + term
                s["wgrad"][32 * g : 32 * g + 32, 192 * n : 192 * n + 192] = total[:, 0:192]
    s["wgrad"][:, 1728:2048] = jnp.zeros((64, 320), F32)
    for k in range(16):
        start = 108 * k
        base = start // 128 * 128
        shift = (256 - (start - base)) % 256
        v = s["wgrad"][:, base : base + 256]
        v = pltpu.roll(v, shift, 1)[:, 0:128] if shift else v[:, 0:128]
        core, y, zlo = k % 2, (k // 2) % 4, k // 8
        for g in range(2):
            s["cpart"][core, g * 2 + zlo, y] = v[32 * g : 32 * g + 32, :]


def body(
    x_hbm, cw_hbm, gamma_ref, beta_ref, hw_hbm, hb_ref, pw_hbm, pb_ref,
    total_ref, cg_ref,
    x, cw, hw, pw, wl, gb,
    own, rim_out, rim_in, field, wall, gall, rims, pick,
    xt, wf, gam, gamt, beta, hwt, pwt, hbt, pbt,
    conv, inv, normed, hidden, gate, dparams, dtargets, dpre, dconv, taps, wgrad,
    part, cpart, r1, r2, r3, q1, q2, q3, q4,
    local_sem, xs, xr, as_, ar, bs, br, gs, gr, cs, cr,
):
    place = Place()
    lon, lat, chi = place.lon, place.lat, place.ch
    core, c1, c2, z, y = place.core, place.c1, place.c2, place.z, place.y
    partner = (lon, lat, 1 - chi)
    sibling = place.sibling()
    other = 1 - chi
    loads = [
        pltpu.make_async_copy(src, dst, local_sem.at[n])
        for n, (src, dst) in enumerate(((x_hbm, x), (cw_hbm, cw), (hw_hbm, hw), (pw_hbm, pw)))
    ]
    for copy in loads:
        copy.start()
    barrier, count = enter(place)
    loads[1].wait()
    pack_weights(cw, gamma_ref, beta_ref, wl, gb)
    loads[0].wait()
    shuffle_latents(x, own, rim_out)
    pl.semaphore_wait(barrier, count)

    mine = pl.ds(pl.multiple_of(16 * core, 16), 16)
    theirs = pl.ds(pl.multiple_of(16 * (1 - core), 16), 16)
    sends = []

    def start(*copies):
        for copy in copies:
            copy.start()
        sends.extend(copies)
        return copies

    def arrive(copies):
        for copy in copies:
            copy.wait_recv()

    start(
        remote(wl.at[mine], wall.at[chi, mine], xs.at[4], xr.at[4], partner),
        remote(gb, gall.at[chi], xs.at[5], xr.at[5], partner),
    )
    down, up = (lat + 3) % 4, (lat + 1) % 4
    for side in range(2):
        near = (lon + 1) % 16 if side == 0 else (lon + 15) % 16
        for kind, (row, half) in enumerate(((lat, 0), (lat, 1), (down, 1), (up, 0))):
            slot = 9 + (side * 2 + kind // 2) * 2
            start(
                remote(
                    rim_out, rim_in.at[side, kind // 2, chi],
                    xs.at[9 + side * 4 + kind], xr.at[slot + chi], (near, row, half),
                )
            )
    start(
        remote(own.at[:, 0], field.at[:, chi, 9], xs.at[7], xr.at[7 + chi], (lon, down, 1)),
        remote(own.at[:, 15], field.at[:, chi, 0], xs.at[8], xr.at[7 + chi], (lon, up, 0)),
    )
    for level in range(4):
        start(
            remote(
                own.at[level, pl.ds(7 * other, 9)], field.at[level, chi, pl.ds(chi, 9)],
                xs.at[level], xr.at[level], partner,
            )
        )
    for level in range(4):
        field[level, chi, pl.ds(other, 9)] = own[level, pl.ds(7 * chi, 9)]
    wall[chi] = wl[...]
    gall[chi] = gb[...]
    loads[2].wait()
    loads[3].wait()
    prepare_small(hw, hb_ref, pw, pb_ref, hwt, pwt, hbt, pbt)
    pick[...] = window_pick()
    remote(gb, gall.at[other], xs.at[5], xr.at[5], partner).wait_recv()
    remote(wl.at[mine], wall.at[other, mine], xs.at[4], xr.at[4], partner).wait_recv()
    start(remote(wall.at[other, mine], wall.at[other, mine], xs.at[6], xr.at[6], sibling))
    build_gamma(gall, gam, gamt, beta)
    for half in range(2):
        remote(
            own.at[:, 0], field.at[:, half, 9 * chi], xs.at[7], xr.at[7 + half], partner
        ).wait_recv()
    for side in range(2):
        for kind in range(2):
            for half in range(2):
                remote(
                    rim_out, rim_in.at[side, kind, half], xs.at[9],
                    xr.at[9 + (side * 2 + kind) * 2 + half], partner,
                ).wait_recv()
    place_rims(place, rim_in, rims)
    remote(
        wall.at[other, mine], wall.at[other, theirs], xs.at[6], xr.at[6], sibling
    ).wait_recv()
    build_weights(wall, wf)

    @pl.when(jnp.where(chi == 0, lat, 3 - lat) == 0)
    def _():
        field[:, :, pl.ds(9 * chi, 1)] = jnp.zeros((4, 2, 1, 32, 128), BF)

    s = {
        "xt": xt, "wf": wf, "gam": gam, "gamt": gamt, "beta": beta, "hwt": hwt, "pwt": pwt,
        "hbt": hbt, "pbt": pbt, "conv": conv, "inv": inv, "normed": normed, "hidden": hidden,
        "gate": gate, "dparams": dparams, "dtargets": dtargets, "dpre": dpre, "dconv": dconv,
        "taps": taps, "wgrad": wgrad, "part": part, "cpart": cpart,
    }
    for level in range(4):
        remote(
            own.at[level, pl.ds(0, 9)], field.at[level, other, pl.ds(other, 9)],
            xs.at[level], xr.at[level], partner,
        ).wait_recv()
        build_windows(field, rims, pick, xt, level)
        if level >= 1:
            forward(s, level - 1)
    forward(s, 3)
    entropy_forward(s)

    spans = (pl.ds(0, 10), pl.ds(10, 6))
    p = c2 * 4 + z

    def core_stage(n):
        return start(
            remote(part.at[1 - core, :, spans[n]], r1.at[:, spans[n]], as_.at[n], ar.at[n], sibling)
        )

    def core_add(n):
        part[core, :, spans[n]] = part[core, :, spans[n]] + r1[:, spans[n]]

    def axis_stage(n):
        return start(
            *[
                remote(
                    part.at[core, (c1 + d) % 4, spans[n]], r2.at[d - 1, spans[n]],
                    as_.at[1 + 3 * n + d], ar.at[1 + 3 * n + d], place.along_first(d),
                )
                for d in (1, 2, 3)
            ]
        )

    def axis_add(n):
        part[core, c1, spans[n]] = (part[core, c1, spans[n]] + r2[0, spans[n]]) + (
            r2[1, spans[n]] + r2[2, spans[n]]
        )

    owners = (range(0, 10), range(10, 16))

    def apart(o, act):
        pl.when(p != o)(act)

    def plane_copy(o):
        return remote(
            part.at[core, c1, o], r3.at[p], bs.at[o], br.at[p], place.in_plane(o // 4, o % 4)
        )

    def plane_stage(n):
        for o in owners[n]:
            apart(o, lambda o=o: plane_copy(o).start())

    def spread_copy(o):
        view = total_ref.at[core, c1, p]
        return remote(view, view, gs.at[o], gr.at[p], place.in_plane(o // 4, o % 4))

    def plane_finish(n):
        @pl.when((p < 10) if n == 0 else (p >= 10))
        def _():
            r3[p] = part[core, c1, p]
            for o in range(16):
                apart(
                    o,
                    lambda o=o: remote(
                        part.at[core, c1, o], r3.at[o], bs.at[o], br.at[o], sibling
                    ).wait_recv(),
                )
            terms = [r3[o] for o in range(16)]
            while len(terms) > 1:
                terms = [terms[k] + terms[k + 1] for k in range(0, len(terms), 2)]
            total_ref[core, c1, p] = terms[0]
            for o in range(16):
                apart(o, lambda o=o: spread_copy(o).start())

    def spread_finish(n):
        for o in owners[n]:
            apart(
                o,
                lambda o=o: remote(
                    part.at[core, c1, o], total_ref.at[core, c1, o], gs.at[o], gr.at[o], sibling
                ).wait_recv(),
            )

    def axis_spread(n):
        view = total_ref.at[core, c1, spans[n]]
        return start(
            *[
                remote(
                    view, view, as_.at[7 + 3 * n + d], ar.at[7 + 3 * n + d], place.along_first(d)
                )
                for d in (1, 2, 3)
            ]
        )

    def axis_arrive(n):
        for d in (1, 2, 3):
            remote(
                total_ref.at[core, c1, spans[n]],
                total_ref.at[core, (c1 + 4 - d) % 4, spans[n]],
                as_.at[7 + 3 * n + d], ar.at[7 + 3 * n + d], sibling,
            ).wait_recv()

    def core_spread(n):
        view = total_ref.at[core, :, spans[n]]
        start(remote(view, view, as_.at[14 + n], ar.at[14 + n], sibling))

    def core_arrive(n):
        remote(
            total_ref.at[core, :, spans[n]], total_ref.at[1 - core, :, spans[n]],
            as_.at[14 + n], ar.at[14 + n], sibling,
        ).wait_recv()

    going = core_stage(0)
    entropy_backward(s, pw)
    arrive(going)
    core_add(0)
    going_axis = axis_stage(0)
    hidden_grads(s)
    going = core_stage(1)
    conv_backward(s, hw)
    arrive(going)
    core_add(1)
    going_axis1 = axis_stage(1)
    weight_grads(s)
    going = start(remote(cpart.at[1 - core], q1, cs.at[0], cr.at[0], sibling))
    arrive(going_axis)
    axis_add(0)
    plane_stage(0)
    arrive(going)
    cpart[core] = cpart[core] + q1[...]
    going = start(
        *[
            remote(
                cpart.at[core, (z + d) % 4], q2.at[d - 1], cs.at[d], cr.at[d], place.along_z(d)
            )
            for d in (1, 2, 3)
        ]
    )
    arrive(going_axis1)
    axis_add(1)
    plane_stage(1)
    plane_finish(0)
    arrive(going)
    cpart[core, z] = (cpart[core, z] + q2[0]) + (q2[1] + q2[2])
    going = start(
        *[
            remote(
                cpart.at[core, z, (y + d) % 4], q3.at[d - 1], cs.at[3 + d], cr.at[3 + d],
                place.along_y(d),
            )
            for d in (1, 2, 3)
        ]
    )
    plane_finish(1)
    spread_finish(0)
    axis_spread(0)
    arrive(going)
    cpart[core, z, y] = (cpart[core, z, y] + q3[0]) + (q3[1] + q3[2])
    going = start(
        *[
            remote(
                cpart.at[core, z, y], q4.at[d - 1], cs.at[6 + d], cr.at[6 + d], place.along_x(d)
            )
            for d in (1, 2, 3)
        ]
    )
    spread_finish(1)
    axis_spread(1)
    axis_arrive(0)
    core_spread(0)
    arrive(going)
    block = (cpart[core, z, y] + q4[0]) + (q4[1] + q4[2])
    cg_ref[...] = pltpu.roll(block, (128 - 27 * place.x) % 128, 1)
    axis_arrive(1)
    core_spread(1)
    core_arrive(0)
    core_arrive(1)
    for copy in sends:
        copy.wait_send()
    for o in range(16):
        apart(o, lambda o=o: plane_copy(o).wait_send())
        apart(o, lambda o=o: spread_copy(o).wait_send())


def unpack(total_ref, block_ref, cg_ref, hwg_ref, hbg_ref, pwg_ref, pbg_ref):
    cg_ref[...] = block_ref[:, 0:27]
    for half in range(2):
        for k in range(4):
            pwg_ref[160 * k : 160 * k + 160, 128 * half : 128 * half + 128] = total_ref[
                half, k, 0:10
            ].reshape(160, 128)
    for n in range(8):
        for k in range(5):
            hwg_ref[16 * n : 16 * n + 16, 128 * k : 128 * k + 128] = total_ref[
                n // 4, n % 4, 10 + k
            ]
    for k in range(5):
        hbg_ref[128 * k : 128 * k + 128] = total_ref[0, 0, 15, k]
    for k in range(2):
        pbg_ref[128 * k : 128 * k + 128] = total_ref[0, 0, 15, 5 + k]


def on_device(x, cw, gamma, beta, hw, hb, pw, pb):
    vmem = pltpu.VMEM
    dma = pltpu.SemaphoreType.DMA
    scratch = [
        vmem((4, 32, 16, 128), BF),
        vmem((27, 32, 64), BF),
        vmem((128, 640), BF),
        vmem((640, 256), BF),
        vmem((32, 1792), BF),
        vmem((32, 128), F32),
        vmem((4, 16, 32, 128), BF),
        vmem((32, 128), BF),
        vmem((2, 2, 2, 32, 128), BF),
        vmem((4, 2, 10, 32, 128), BF),
        vmem((2, 32, 1792), BF),
        vmem((2, 32, 128), F32),
        vmem((64, 128), F32),
        vmem((384, 512), BF),
        vmem((1024, 1024), BF),
        vmem((3, 256, 1024), BF),
        vmem((2, 256, 256), F32),
        vmem((2, 256, 256), F32),
        vmem((256, 256), F32),
        vmem((640, 128), BF),
        vmem((256, 640), BF),
        vmem((640, 128), F32),
        vmem((256, 128), F32),
        vmem((256, 1024), F32),
        vmem((256, 1024), F32),
        vmem((256, 1024), BF),
        vmem((640, 1024), BF),
        vmem((640, 1024), F32),
        vmem((256, 1024), BF),
        vmem((128, 1024), BF),
        vmem((640, 1024), BF),
        vmem((256, 1024), BF),
        vmem((3, 256, 1024), F32),
        vmem((64, 2048), F32),
        vmem((2, 4, 16, 16, 128), F32),
        vmem((2, 4, 4, 32, 128), F32),
        vmem((4, 16, 16, 128), F32),
        vmem((3, 16, 16, 128), F32),
        vmem((16, 16, 128), F32),
        vmem((4, 4, 32, 128), F32),
        vmem((3, 4, 32, 128), F32),
        vmem((3, 32, 128), F32),
        vmem((3, 32, 128), F32),
        dma((4,)),
        dma((17,)),
        dma((17,)),
        dma((16,)),
        dma((16,)),
        dma((16,)),
        dma((16,)),
        dma((16,)),
        dma((16,)),
        dma((10,)),
        dma((10,)),
    ]
    spec = pl.BlockSpec(memory_space=pltpu.VMEM)
    anywhere = pl.BlockSpec(memory_space=pl.ANY)
    total, block = pl.pallas_call(
        body,
        out_shape=(
            jax.ShapeDtypeStruct((2, 4, 16, 16, 128), F32),
            jax.ShapeDtypeStruct((32, 128), F32),
        ),
        in_specs=[anywhere, anywhere, spec, spec, anywhere, spec, anywhere, spec],
        out_specs=(spec, spec),
        scratch_shapes=scratch,
        compiler_params=pltpu.CompilerParams(
            collective_id=0, has_side_effects=True, vmem_limit_bytes=56 * 1024 * 1024
        ),
    )(x, jnp.transpose(cw, (1, 0, 2)), gamma, beta, hw, hb, pw, pb)
    return pl.pallas_call(
        unpack,
        out_shape=(
            jax.ShapeDtypeStruct((32, 27), F32),
            jax.ShapeDtypeStruct((128, 640), F32),
            jax.ShapeDtypeStruct((640,), F32),
            jax.ShapeDtypeStruct((640, 256), F32),
            jax.ShapeDtypeStruct((256,), F32),
        ),
        in_specs=[spec] * 2,
        out_specs=(spec,) * 5,
    )(total, block)


def solution(mesh):
    placed = (
        P(None, "ch", "lat", "lon"),
        P("ch", None, None),
        P("ch", None),
        P("ch"),
        P(),
        P(),
        P(),
        P(),
    )
    return jax.shard_map(
        on_device,
        mesh=mesh,
        in_specs=placed,
        out_specs=(P("ch", ("lon", "lat")), P(), P(), P(), P()),
        check_vma=False,
    )
```

```python
import jax
import jax.numpy as jnp
from jax import lax
from jax.experimental import pallas as pl
from jax.experimental.pallas import tpu as pltpu
from jax.sharding import PartitionSpec as P

BF = jnp.bfloat16
F32 = jnp.float32
MESH = pl.DeviceIdType.MESH
PATCHES = 131072.0
OFFSETS = [(a, b) for a in range(4) for b in range(4) if a or b]

NN = (((1,), (0,)), ((), ()))
NT = (((1,), (1,)), ((), ()))


def mm(a, b, dims=NN):
    return lax.dot_general(a, b, dims, preferred_element_type=F32)


def iota(shape, dim):
    return lax.broadcasted_iota(jnp.int32, shape, dim)


def onehot(condition):
    return jnp.where(condition, 1.0, 0.0).astype(BF)


def tile_spot(t):
    core, rest = divmod(t, 40)
    return core, rest // 3, 8 * (rest % 3)


def split(value):
    high = value.astype(BF)
    return high, (value - high.astype(F32)).astype(BF)


class Place:
    def __init__(self):
        self.lon = lax.axis_index("lon")
        self.lat = lax.axis_index("lat")
        self.ch = lax.axis_index("ch")
        self.core = self.lon % 2
        self.y = (self.lon // 2) % 4
        self.zlo = self.lon // 8
        self.x = self.lat
        self.z = self.ch * 2 + self.zlo

    def chip(self, x, y, z, core):
        return ((z % 2) * 8 + y * 2 + core, x, z // 2)

    def sibling(self):
        return self.chip(self.x, self.y, self.z, 1 - self.core)

    def along_z(self, d):
        return self.chip(self.x, self.y, (self.z + d) % 4, self.core)

    def flat(self, a, b):
        return self.chip((self.x + a) % 4, (self.y + b) % 4, self.z, self.core)

    def plane(self, n, a, b):
        if n == 1:
            return self.chip((self.x + a) % 4, self.y, (self.z + b) % 4, self.core)
        on, off = 1 - self.core, self.core
        x = (self.x + a * on) % 4
        y = (self.y + b * on + a * off) % 4
        z = (self.z + b * off) % 4
        return self.chip(x, y, z, self.core)

    def spot(self, n, a=0, b=0):
        if n == 1:
            return ((self.x + a) % 4) * 4 + (self.z + b) % 4
        first = jnp.where(self.core == 0, self.x, self.y)
        second = jnp.where(self.core == 0, self.y, self.z)
        return ((first + a) % 4) * 4 + (second + b) % 4

    def axis(self, n):
        return self.y if n == 1 else jnp.where(self.core == 0, self.z, self.x)

    def along(self, n, d):
        if n == 1:
            return self.flat(0, d)
        on, off = 1 - self.core, self.core
        return self.chip((self.x + d * off) % 4, self.y, (self.z + d * on) % 4, self.core)


def remote(src, dst, send, recv, device):
    return pltpu.make_async_remote_copy(
        src_ref=src,
        dst_ref=dst,
        send_sem=send,
        recv_sem=recv,
        device_id=device,
        device_id_type=MESH,
    )


def enter(place):
    lon, lat, ch = place.lon, place.lat, place.ch
    barrier = pltpu.get_barrier_semaphore()
    row = (lat + 2 * ch + 3) % 4
    devices = [(lon, lat, 1 - ch), (lon, row, 0), (lon, row, 1)]
    for side in (1, 15):
        for other in (0, 1):
            devices.append(((lon + side) % 16, lat, other))
            devices.append(((lon + side) % 16, row, other))
    devices.append(place.sibling())
    devices += [place.along_z(d) for d in (1, 2, 3)]
    devices += [place.flat(a, b) for a, b in OFFSETS]
    devices += [place.plane(1, a, b) for a, b in OFFSETS if a and b]
    for device in devices:
        pl.semaphore_signal(barrier, inc=1, device_id=device, device_id_type=MESH)

    @pl.when(place.core == 1)
    def _():
        for a, b in OFFSETS:
            if a and b:
                pl.semaphore_signal(
                    barrier, inc=1, device_id=place.plane(0, a, b), device_id_type=MESH
                )

    return barrier, len(devices) + 9 * place.core


def shuffle_latents(x_ref, own, rim_out):
    rows, cols = iota((512, 512), 0), iota((512, 512), 1)
    swap = onehot(cols == ((rows & 31) << 4) + (rows >> 5))
    b, n = iota((128, 256), 0), iota((128, 256), 1)
    parity = jnp.where(n < 64, 2 * n, 2 * n - 127)
    edge = jnp.where(n < 192, 0, 127)
    spread = onehot(b == jnp.where(n < 128, parity, edge))
    r, j = iota((512, 128), 0), iota((512, 128), 1)
    slot = (j & 63) - ((r & 15) << 2)
    rims = jnp.zeros((512, 128), F32)
    for pair in range(2):
        blocks = []
        for level in (2 * pair, 2 * pair + 1):
            block = mm(x_ref[level].reshape(512, 128), spread)
            rims = jnp.where(slot == level, block[:, 128:], rims)
            blocks.append(block[:, :128].astype(BF))
        moved = mm(swap, jnp.concatenate(blocks, axis=1)).astype(BF)
        own[2 * pair] = moved[:, :128].reshape(16, 32, 128)
        own[2 * pair + 1] = moved[:, 128:].reshape(16, 32, 128)
    c, k = iota((32, 512), 0), iota((32, 512), 1)
    rim_out[...] = mm(onehot((k >> 4) == c), rims.astype(BF)).astype(BF)


def pack_weights(cw_ref, gamma_ref, beta_ref, wl, gb):
    for k in range(13):
        wl[:, 128 * k : 128 * k + 128] = jnp.concatenate(
            [cw_ref[2 * k].astype(F32), cw_ref[2 * k + 1].astype(F32)], axis=1
        ).astype(BF)
    wl[:, 1664:1792] = jnp.concatenate(
        [cw_ref[26].astype(F32), jnp.zeros((32, 64), F32)], axis=1
    ).astype(BF)
    line = beta_ref[...].reshape(1, 32)
    column = jnp.sum(
        jnp.where(iota((32, 32), 0) == iota((32, 32), 1), line, 0.0), axis=1, keepdims=True
    )
    gb[:, 0:32] = gamma_ref[...]
    gb[:, 32:128] = jnp.broadcast_to(column, (32, 96))


def prepare_small(hw, hb_ref, pw, pb_ref, hwt, pwt, hbt, pbt):
    eye = onehot(iota((128, 128), 0) == iota((128, 128), 1))
    for k in range(5):
        part = slice(128 * k, 128 * k + 128)
        hwt[part, :] = mm(eye, hw[:, part], NT).astype(BF)
        hbt[part, :] = jnp.broadcast_to(hb_ref[part].reshape(1, 128), (128, 128)).T
    for k in range(2):
        part = slice(128 * k, 128 * k + 128)
        pwt[part, :] = mm(eye, pw[:, part], NT).astype(BF)
        pbt[part, :] = jnp.broadcast_to(pb_ref[part].reshape(1, 128), (128, 128)).T


def build_gamma(gall, gam, gamt, beta):
    k, n = iota((128, 256), 0), iota((128, 256), 1)
    copies = onehot(k == (n & 31))
    for g in range(2):
        high, low = split(gall[g])
        for which, part in ((0, high), (1, low)):
            wide = mm(part, copies)
            for s in range(4):
                block = g * 4 + s
                own_block = (iota((32, 256), 1) >> 5) == block
                gam[which, block * 32 : block * 32 + 32, :] = jnp.where(own_block, wide, 0.0)
        for s in range(4):
            block = g * 4 + s
            beta[block * 32 : block * 32 + 32, :] = jnp.broadcast_to(
                gall[g][:, 64:65], (32, 256)
            )
    for which in range(2):
        gamt[which] = gam[which].T


def build_weights(wall, wf):
    lane = iota((32, 256), 1)
    for g in range(2):
        for n in range(9):
            dl, da = n // 3, n % 3
            base = (192 * n) // 128 * 128
            v = wall[g, :, base : base + 256].astype(F32)
            first = v if n % 2 == 0 else pltpu.roll(v, 192, 1)
            second = v if n % 2 == 1 else pltpu.roll(v, 64, 1)
            first = jnp.where(lane < 192, first, 0.0).astype(BF)
            second = jnp.where(lane >= 64, second, 0.0).astype(BF)
            for p in range(2):
                r = da + p
                row = g * 128 + 2 * p * 32
                wf[dl, row : row + 32, 256 * r : 256 * r + 256] = first
                wf[dl, row + 32 : row + 64, 256 * r : 256 * r + 256] = second
        for dl in range(3):
            for p in range(2):
                r = 3 if p == 0 else 0
                row = g * 128 + 2 * p * 32
                wf[dl, row : row + 64, 256 * r : 256 * r + 256] = jnp.zeros((64, 256), BF)


def place_rims(place, rim_in, rims):
    chi, lat = place.ch, place.lat
    k, n = iota((512, 128), 0), iota((512, 128), 1)
    block, kk, nn = k >> 7, k & 127, n & 63
    left = block < 2
    same = (block & 1) == 0
    pole = jnp.where(chi == 0, lat, 3 - lat) == 0
    shift_same = (8 * chi - 1) * 4
    other_low = 36 * chi
    shift_other = jnp.where(chi == 0, 60, -36)
    shift = jnp.where(same, shift_same, shift_other)
    source = nn + shift
    inside = (source >= 0) & (source < 64) & (nn < 40)
    only = (nn >= other_low) & (nn < other_low + 4) & jnp.logical_not(pole)
    valid = inside & (same | only)
    side = (left & (n < 64)) | (jnp.logical_not(left) & (n >= 64))
    chosen = kk == source + jnp.where(left, 64, 0)
    pick = onehot(valid & side & chosen)
    tiles = jnp.concatenate(
        [rim_in[s, t].reshape(64, 128) for s in range(2) for t in range(2)], axis=1
    )
    rims[...] = mm(tiles, pick)


def window_pick():
    col = iota((1, 512), 1)
    w, js, m = col >> 7, (col & 127) >> 6, col & 63
    target = jnp.where(
        w == 0,
        jnp.where(m == 0, 256 + js * 8, js * 128 + 63 + m),
        jnp.where(
            w == 1,
            js * 128 + m,
            jnp.where(
                w == 2,
                js * 128 + 64 + m,
                jnp.where(m == 63, 320 + js * 8, js * 128 + m + 1),
            ),
        ),
    )
    return onehot(iota((384, 512), 0) == target)


def build_windows(field, rims, pick, xt, level):
    stack = []
    for r in range(4):
        for pair in range(2):
            j0 = r + 4 * pair
            edge = pltpu.roll(rims[...], 128 - (j0 * 4 + level), 1).astype(BF)
            rows = [field[level, :, j].reshape(64, 128) for j in (j0, j0 + 2)]
            stack.append(jnp.concatenate(rows + [edge], axis=1))
    out = mm(jnp.concatenate(stack, axis=0), pick[...]).astype(BF)
    for r in range(4):
        for pair in range(2):
            row, lane = (r * 2 + pair) * 64, level * 256 + pair * 128
            for v in range(4):
                xt[r * 256 + v * 64 : r * 256 + v * 64 + 64, lane : lane + 128] = out[
                    row : row + 64, v * 128 : v * 128 + 128
                ]


def mix(gam, value):
    high, low = split(value)
    ghigh, glow = gam[0].astype(BF), gam[1].astype(BF)
    return mm(ghigh, high) + (mm(ghigh, low) + mm(glow, high))


def forward(s, level):
    lanes = slice(256 * level, 256 * level + 256)
    total = None
    for dl in range(3):
        other = level + dl - 1
        if 0 <= other < 4:
            term = mm(s["wf"][dl], s["xt"][:, 256 * other : 256 * other + 256])
            total = term if total is None else total + term
    s["conv"][:, lanes] = total
    inv = lax.rsqrt(s["beta"][...] + mix(s["gam"], total * total))
    s["inv"][:, lanes] = inv
    s["normed"][:, lanes] = (total * inv).astype(BF)


def entropy_forward(s):
    def first(i, carry):
        lanes = pl.ds(pl.multiple_of(i * 256, 256), 256)
        features = s["normed"][0:128, lanes]
        for k in range(5):
            part = slice(128 * k, 128 * k + 128)
            bias = s["hbt"][part, :]
            pre = mm(s["hwt"][part, :], features) + jnp.concatenate([bias, bias], axis=1)
            sig = 0.5 * jnp.tanh(0.5 * pre) + 0.5
            act = pre * sig
            s["hidden"][part, lanes] = act.astype(BF)
            s["gate"][part, lanes] = sig * (1.0 + pre - act)
        return carry

    lax.fori_loop(0, 4, first, 0)

    def second(i, carry):
        lanes = pl.ds(pl.multiple_of(i * 256, 256), 256)
        hidden = s["hidden"][:, lanes]
        cb, rb = s["pbt"][0:128, :], s["pbt"][128:256, :]
        centre = mm(s["pwt"][0:128, :], hidden) + jnp.concatenate([cb, cb], axis=1)
        raw = mm(s["pwt"][128:256, :], hidden) + jnp.concatenate([rb, rb], axis=1)
        small = jnp.exp(-jnp.abs(raw))
        spread = 0.5 + jnp.maximum(raw, 0.0) + jnp.log(1.0 + small)
        fraction = 1.0 / (1.0 + small)
        sig = jnp.where(raw >= 0.0, fraction, small * fraction)
        over = 1.0 / spread
        error = (s["normed"][128:256, lanes].astype(F32) - centre) * over
        ratio = error * over * (1.0 / PATCHES)
        s["dparams"][0:128, lanes] = (-ratio).astype(BF)
        s["dparams"][128:256, lanes] = (
            (1.0 - error * error) * over * sig * (1.0 / PATCHES)
        ).astype(BF)
        s["dtargets"][:, lanes] = ratio.astype(BF)
        return carry

    lax.fori_loop(0, 4, second, 0)

    grad = mm(s["hidden"][...], s["dparams"][...], NT)
    for half in range(2):
        s["ppart"][half] = grad[:, 128 * half : 128 * half + 128].reshape(16, 40, 128)


def entropy_backward(s, pw):
    def third(i, carry):
        lanes = pl.ds(pl.multiple_of(i * 256, 256), 256)
        back = mm(pw[...], s["dparams"][:, lanes])
        s["dpre"][:, lanes] = (back * s["gate"][:, lanes]).astype(BF)
        return carry

    lax.fori_loop(0, 4, third, 0)


def hidden_grads(s):
    hpart = s["hpart"]
    ones = jnp.ones((8, 1024), BF)
    pb = mm(ones, s["dparams"][...], NT)
    grad = mm(s["normed"][0:128, :], s["dpre"][...], NT)
    hb = mm(ones, s["dpre"][...], NT)
    zeros = jnp.zeros((1, 128), F32)
    lines = [hb[0:1, 128 * k : 128 * k + 128] for k in range(5)]
    lines += [pb[0:1, 0:128], pb[0:1, 128:256], zeros]
    for t in range(80):
        core, place, row = tile_spot(t)
        n, k = t // 5, t % 5
        hpart[core, place, row : row + 8] = grad[8 * n : 8 * n + 8, 128 * k : 128 * k + 128]
    hpart[0, 13, 8:16] = jnp.concatenate(lines, axis=0)
    hpart[1, 13, 8:16] = jnp.zeros((8, 128), F32)
    for core in range(2):
        hpart[core, 13, 16:24] = jnp.zeros((8, 128), F32)
        hpart[core, 14:16] = jnp.zeros((2, 24, 128), F32)


def conv_backward(s, hw):
    for level in range(4):
        lanes = slice(256 * level, 256 * level + 256)
        dfeat = mm(hw[...], s["dpre"][:, lanes]).astype(BF).astype(F32)
        dn = jnp.concatenate([dfeat, s["dtargets"][:, lanes].astype(F32)], axis=0)
        inv = s["inv"][:, lanes]
        y = s["conv"][:, lanes]
        dni = dn * inv
        weighted = dni * y * (inv * inv)
        s["dconv"][:, lanes] = (dni - y * mix(s["gamt"], weighted)).astype(BF)


def weight_grads(s):
    for dl in range(3):
        first, last = max(0, 1 - dl), min(4, 5 - dl)
        d = s["dconv"][:, 256 * first : 256 * last]
        x = s["xt"][:, 256 * (first + dl - 1) : 256 * (last + dl - 1)]
        s["taps"][dl] = mm(d, x, NT)
    for dl in range(3):
        for da in range(3):
            n = dl * 3 + da
            for g in range(2):
                total = None
                for p in range(2):
                    row = g * 128 + 2 * p * 32
                    lanes = slice(256 * (da + p), 256 * (da + p) + 256)
                    a = s["taps"][dl, row : row + 32, lanes]
                    b = s["taps"][dl, row + 32 : row + 64, lanes]
                    term = a + pltpu.roll(b, 192, 1)
                    total = term if total is None else total + term
                s["wgrad"][32 * g : 32 * g + 32, 192 * n : 192 * n + 192] = total[:, 0:192]
    s["wgrad"][:, 1728:2048] = jnp.zeros((64, 320), F32)
    lane = iota((8, 128), 1) >> 5
    for k in range(64):
        first = 27 * k
        base = first // 128 * 128
        offset = first - base
        wide = 128 if offset <= 101 else 256
        lon, x = k // 4, k % 4
        core, y, zlo = lon % 2, (lon // 2) % 4, lon // 8
        for g in range(2):
            tile = None
            for q in range(4):
                v = s["wgrad"][32 * g + 8 * q : 32 * g + 8 * q + 8, base : base + wide]
                shift = (32 * q - offset) % wide
                v = pltpu.roll(v, shift, 1)[:, 0:128] if shift else v[:, 0:128]
                tile = v if tile is None else jnp.where(lane == q, v, tile)
            s["cpart"][core, g * 2 + zlo, y, x] = tile


def body(
    x_hbm, cw_hbm, gamma_ref, beta_ref, hw_hbm, hb_ref, pw_hbm, pb_ref,
    ptotal, htotal, cg_ref,
    x, cw, hw, pw, wl, gb,
    own, rim_out, rim_in, field, wall, gall, rims, pick,
    xt, wf, gam, gamt, beta, hwt, pwt, hbt, pbt,
    conv, inv, normed, hidden, gate, dparams, dtargets, dpre, dconv, taps, wgrad,
    ppart, hpart, cpart, pr1, hr1, pr2, hr2, pr3, hr3, q1, q2, q3,
    local_sem, xs, xr, ks, kr, bs, br, es, er, gs, gr, cs, cr,
):
    place = Place()
    lon, lat, chi = place.lon, place.lat, place.ch
    core, z, y = place.core, place.z, place.y
    partner = (lon, lat, 1 - chi)
    sibling = place.sibling()
    other = 1 - chi
    loads = [
        pltpu.make_async_copy(src, dst, local_sem.at[n])
        for n, (src, dst) in enumerate(((x_hbm, x), (cw_hbm, cw), (hw_hbm, hw), (pw_hbm, pw)))
    ]
    for copy in loads:
        copy.start()
    barrier, count = enter(place)
    loads[1].wait()
    pack_weights(cw, gamma_ref, beta_ref, wl, gb)
    loads[0].wait()
    shuffle_latents(x, own, rim_out)
    pl.semaphore_wait(barrier, count)

    mine = pl.ds(pl.multiple_of(16 * core, 16), 16)
    theirs = pl.ds(pl.multiple_of(16 * (1 - core), 16), 16)
    sends = []

    def start(*copies):
        for copy in copies:
            copy.start()
        sends.extend(copies)
        return copies

    def arrive(copies):
        for copy in copies:
            copy.wait_recv()

    start(
        remote(wl.at[mine], wall.at[chi, mine], xs.at[4], xr.at[4], partner),
        remote(gb, gall.at[chi], xs.at[5], xr.at[5], partner),
    )
    down, up = (lat + 3) % 4, (lat + 1) % 4
    for side in range(2):
        near = (lon + 1) % 16 if side == 0 else (lon + 15) % 16
        for kind, (row, half) in enumerate(((lat, 0), (lat, 1), (down, 1), (up, 0))):
            slot = 9 + (side * 2 + kind // 2) * 2
            start(
                remote(
                    rim_out, rim_in.at[side, kind // 2, chi],
                    xs.at[9 + side * 4 + kind], xr.at[slot + chi], (near, row, half),
                )
            )
    start(
        remote(own.at[:, 0], field.at[:, chi, 9], xs.at[7], xr.at[7 + chi], (lon, down, 1)),
        remote(own.at[:, 15], field.at[:, chi, 0], xs.at[8], xr.at[7 + chi], (lon, up, 0)),
    )
    levels = [
        remote(
            own.at[level, pl.ds(7 * other, 9)], field.at[level, chi, pl.ds(chi, 9)],
            xs.at[level], xr.at[level], partner,
        )
        for level in range(4)
    ]
    levels[0].start()
    levels[1].start()
    for level in range(4):
        field[level, chi, pl.ds(other, 9)] = own[level, pl.ds(7 * chi, 9)]
    wall[chi] = wl[...]
    gall[chi] = gb[...]
    loads[2].wait()
    loads[3].wait()
    prepare_small(hw, hb_ref, pw, pb_ref, hwt, pwt, hbt, pbt)
    pick[...] = window_pick()
    remote(gb, gall.at[other], xs.at[5], xr.at[5], partner).wait_recv()
    remote(wl.at[mine], wall.at[other, mine], xs.at[4], xr.at[4], partner).wait_recv()
    start(remote(wall.at[other, mine], wall.at[other, mine], xs.at[6], xr.at[6], sibling))
    levels[0].wait_send()
    levels[2].start()
    build_gamma(gall, gam, gamt, beta)
    levels[1].wait_send()
    levels[3].start()
    for half in range(2):
        remote(
            own.at[:, 0], field.at[:, half, 9 * chi], xs.at[7], xr.at[7 + half], partner
        ).wait_recv()
    for side in range(2):
        for kind in range(2):
            for half in range(2):
                remote(
                    rim_out, rim_in.at[side, kind, half], xs.at[9],
                    xr.at[9 + (side * 2 + kind) * 2 + half], partner,
                ).wait_recv()
    place_rims(place, rim_in, rims)
    remote(
        wall.at[other, mine], wall.at[other, theirs], xs.at[6], xr.at[6], sibling
    ).wait_recv()
    build_weights(wall, wf)

    @pl.when(jnp.where(chi == 0, lat, 3 - lat) == 0)
    def _():
        field[:, :, pl.ds(9 * chi, 1)] = jnp.zeros((4, 2, 1, 32, 128), BF)

    s = {
        "xt": xt, "wf": wf, "gam": gam, "gamt": gamt, "beta": beta, "hwt": hwt, "pwt": pwt,
        "hbt": hbt, "pbt": pbt, "conv": conv, "inv": inv, "normed": normed, "hidden": hidden,
        "gate": gate, "dparams": dparams, "dtargets": dtargets, "dpre": dpre, "dconv": dconv,
        "taps": taps, "wgrad": wgrad, "ppart": ppart, "hpart": hpart, "cpart": cpart,
    }
    for level in range(4):
        remote(
            own.at[level, pl.ds(0, 9)], field.at[level, other, pl.ds(other, 9)],
            xs.at[level], xr.at[level], partner,
        ).wait_recv()
        build_windows(field, rims, pick, xt, level)
        if level >= 1:
            forward(s, level - 1)
    sends.extend(levels[2:])
    forward(s, 3)
    entropy_forward(s)

    parts, totals = (ppart, hpart), (ptotal, htotal)
    firsts, seconds, thirds = (pr1, hr1), (pr2, hr2), (pr3, hr3)

    def core_stage(n):
        return start(
            remote(parts[n].at[1 - core], firsts[n], ks.at[n], kr.at[n], sibling)
        )

    def core_add(n):
        parts[n][core] = parts[n][core] + firsts[n][...]

    def plane_stage(n):
        return start(
            *[
                remote(
                    parts[n].at[core, place.spot(n, a, b)], seconds[n].at[4 * a + b],
                    bs.at[n, 4 * a + b], br.at[n, 4 * a + b], place.plane(n, a, b),
                )
                for a, b in OFFSETS
            ]
        )

    def plane_add(n):
        terms = [parts[n][core, place.spot(n)]] + [seconds[n][k] for k in range(1, 16)]
        while len(terms) > 1:
            terms = [terms[k] + terms[k + 1] for k in range(0, len(terms), 2)]
        thirds[n][place.axis(n)] = terms[0]

    def axis_stage(n):
        axis = place.axis(n)
        copies = start(
            *[
                remote(
                    thirds[n].at[axis], thirds[n].at[axis],
                    es.at[n, d], er.at[n, d], place.along(n, d),
                )
                for d in (1, 2, 3)
            ]
        )
        return [
            remote(
                thirds[n].at[axis], thirds[n].at[(axis + 4 - d) % 4],
                es.at[n, d], er.at[n, d], sibling,
            )
            for d in (1, 2, 3)
        ]

    def axis_add(n):
        totals[n][core, place.spot(n)] = (thirds[n][0] + thirds[n][1]) + (thirds[n][2] + thirds[n][3])

    def spread_stage(n):
        view = totals[n].at[core, place.spot(n)]
        start(
            *[
                remote(
                    view, view, gs.at[n, 4 * a + b], gr.at[n, 4 * a + b], place.plane(n, a, b)
                )
                for a, b in OFFSETS
            ]
        )
        return [
            remote(
                view, totals[n].at[core, place.spot(n, 4 - a, 4 - b)],
                gs.at[n, 4 * a + b], gr.at[n, 4 * a + b], sibling,
            )
            for a, b in OFFSETS
        ]

    def core_spread(n):
        view = totals[n].at[core]
        start(remote(view, view, ks.at[2 + n], kr.at[2 + n], sibling))
        return [remote(view, totals[n].at[1 - core], ks.at[2 + n], kr.at[2 + n], sibling)]

    core_p = core_stage(0)
    entropy_backward(s, pw)
    arrive(core_p)
    core_add(0)
    plane_p = plane_stage(0)
    hidden_grads(s)
    core_h = core_stage(1)
    conv_backward(s, hw)
    arrive(core_h)
    core_add(1)
    plane_h = plane_stage(1)
    weight_grads(s)
    core_c = start(remote(cpart.at[1 - core], q1, cs.at[0], cr.at[0], sibling))
    arrive(plane_p)
    plane_add(0)
    axis_p = axis_stage(0)
    arrive(core_c)
    cpart[core] = cpart[core] + q1[...]
    axis_c = start(
        *[
            remote(
                cpart.at[core, (z + d) % 4], q2.at[d - 1], cs.at[d], cr.at[d], place.along_z(d)
            )
            for d in (1, 2, 3)
        ]
    )
    arrive(plane_h)
    plane_add(1)
    axis_h = axis_stage(1)
    arrive(axis_p)
    axis_add(0)
    spread_p = spread_stage(0)
    arrive(axis_h)
    axis_add(1)
    spread_h = spread_stage(1)
    arrive(axis_c)
    cpart[core, z] = (cpart[core, z] + q2[0]) + (q2[1] + q2[2])
    plane_c = start(
        *[
            remote(
                cpart.at[core, z, (y + b) % 4, (place.x + a) % 4], q3.at[4 * a + b],
                cs.at[3 + 4 * a + b],
                cr.at[3 + 4 * a + b], place.flat(a, b),
            )
            for a, b in OFFSETS
        ]
    )
    arrive(spread_p)
    core_p = core_spread(0)
    arrive(spread_h)
    core_h = core_spread(1)
    arrive(plane_c)
    terms = [cpart[core, z, y, place.x]] + [q3[k] for k in range(1, 16)]
    while len(terms) > 1:
        terms = [terms[k] + terms[k + 1] for k in range(0, len(terms), 2)]
    for q in range(4):
        v = pltpu.roll(terms[0], 128 - 32 * q, 1) if q else terms[0]
        cg_ref[8 * q : 8 * q + 8, :] = v
    arrive(core_p)
    arrive(core_h)
    for copy in sends:
        copy.wait_send()


def unpack(ptotal, htotal, block_ref, cg_ref, hwg_ref, hbg_ref, pwg_ref, pbg_ref):
    cg_ref[...] = block_ref[:, 0:27]
    for half in range(2):
        pwg_ref[:, 128 * half : 128 * half + 128] = ptotal[half].reshape(640, 128)
    for t in range(80):
        core, place, row = tile_spot(t)
        n, k = t // 5, t % 5
        hwg_ref[8 * n : 8 * n + 8, 128 * k : 128 * k + 128] = htotal[core, place, row : row + 8]
    for k in range(5):
        hbg_ref[128 * k : 128 * k + 128] = htotal[0, 13, 8 + k]
    for k in range(2):
        pbg_ref[128 * k : 128 * k + 128] = htotal[0, 13, 13 + k]


def on_device(x, cw, gamma, beta, hw, hb, pw, pb):
    vmem = pltpu.VMEM
    dma = pltpu.SemaphoreType.DMA
    scratch = [
        vmem((4, 32, 16, 128), BF),
        vmem((27, 32, 64), BF),
        vmem((128, 640), BF),
        vmem((640, 256), BF),
        vmem((32, 1792), BF),
        vmem((32, 128), F32),
        vmem((4, 16, 32, 128), BF),
        vmem((32, 128), BF),
        vmem((2, 2, 2, 32, 128), BF),
        vmem((4, 2, 10, 32, 128), BF),
        vmem((2, 32, 1792), BF),
        vmem((2, 32, 128), F32),
        vmem((64, 128), F32),
        vmem((384, 512), BF),
        vmem((1024, 1024), BF),
        vmem((3, 256, 1024), BF),
        vmem((2, 256, 256), F32),
        vmem((2, 256, 256), F32),
        vmem((256, 256), F32),
        vmem((640, 128), BF),
        vmem((256, 640), BF),
        vmem((640, 128), F32),
        vmem((256, 128), F32),
        vmem((256, 1024), F32),
        vmem((256, 1024), F32),
        vmem((256, 1024), BF),
        vmem((640, 1024), BF),
        vmem((640, 1024), F32),
        vmem((256, 1024), BF),
        vmem((128, 1024), BF),
        vmem((640, 1024), BF),
        vmem((256, 1024), BF),
        vmem((3, 256, 1024), F32),
        vmem((64, 2048), F32),
        vmem((2, 16, 40, 128), F32),
        vmem((2, 16, 24, 128), F32),
        vmem((2, 4, 4, 4, 8, 128), F32),
        vmem((16, 40, 128), F32),
        vmem((16, 24, 128), F32),
        vmem((16, 40, 128), F32),
        vmem((16, 24, 128), F32),
        vmem((4, 40, 128), F32),
        vmem((4, 24, 128), F32),
        vmem((4, 4, 4, 8, 128), F32),
        vmem((3, 4, 4, 8, 128), F32),
        vmem((16, 8, 128), F32),
        dma((4,)),
        dma((17,)),
        dma((17,)),
        dma((4,)),
        dma((4,)),
        dma((2, 16)),
        dma((2, 16)),
        dma((2, 4)),
        dma((2, 4)),
        dma((2, 16)),
        dma((2, 16)),
        dma((19,)),
        dma((19,)),
    ]
    spec = pl.BlockSpec(memory_space=pltpu.VMEM)
    anywhere = pl.BlockSpec(memory_space=pl.ANY)
    ptotal, htotal, block = pl.pallas_call(
        body,
        out_shape=(
            jax.ShapeDtypeStruct((2, 16, 40, 128), F32),
            jax.ShapeDtypeStruct((2, 16, 24, 128), F32),
            jax.ShapeDtypeStruct((32, 128), F32),
        ),
        in_specs=[anywhere, anywhere, spec, spec, anywhere, spec, anywhere, spec],
        out_specs=(spec, spec, spec),
        scratch_shapes=scratch,
        compiler_params=pltpu.CompilerParams(
            collective_id=0, has_side_effects=True, vmem_limit_bytes=56 * 1024 * 1024
        ),
    )(x, jnp.transpose(cw, (1, 0, 2)), gamma, beta, hw, hb, pw, pb)
    return pl.pallas_call(
        unpack,
        out_shape=(
            jax.ShapeDtypeStruct((32, 27), F32),
            jax.ShapeDtypeStruct((128, 640), F32),
            jax.ShapeDtypeStruct((640,), F32),
            jax.ShapeDtypeStruct((640, 256), F32),
            jax.ShapeDtypeStruct((256,), F32),
        ),
        in_specs=[spec] * 3,
        out_specs=(spec,) * 5,
    )(ptotal, htotal, block)


def solution(mesh):
    placed = (
        P(None, "ch", "lat", "lon"),
        P("ch", None, None),
        P("ch", None),
        P("ch"),
        P(),
        P(),
        P(),
        P(),
    )
    return jax.shard_map(
        on_device,
        mesh=mesh,
        in_specs=placed,
        out_specs=(P("ch", ("lon", "lat")), P(), P(), P(), P()),
        check_vma=False,
    )
```

```python
import jax
import jax.numpy as jnp
from jax import lax
from jax.experimental import pallas as pl
from jax.experimental.pallas import tpu as pltpu
from jax.sharding import PartitionSpec as P

BF = jnp.bfloat16
F32 = jnp.float32
MESH = pl.DeviceIdType.MESH
PATCHES = 131072.0
OFFSETS = [(a, b) for a in range(4) for b in range(4) if a or b]

NN = (((1,), (0,)), ((), ()))
NT = (((1,), (1,)), ((), ()))


def mm(a, b, dims=NN):
    return lax.dot_general(a, b, dims, preferred_element_type=F32)


def iota(shape, dim):
    return lax.broadcasted_iota(jnp.int32, shape, dim)


def onehot(condition):
    return jnp.where(condition, 1.0, 0.0).astype(BF)


def tile_spot(t):
    core, rest = divmod(t, 40)
    return core, rest // 3, 8 * (rest % 3)


def split(value):
    high = value.astype(BF)
    return high, (value - high.astype(F32)).astype(BF)


class Place:
    def __init__(self):
        self.lon = lax.axis_index("lon")
        self.lat = lax.axis_index("lat")
        self.ch = lax.axis_index("ch")
        self.core = self.lon % 2
        self.y = (self.lon // 2) % 4
        self.zlo = self.lon // 8
        self.x = self.lat
        self.z = self.ch * 2 + self.zlo

    def chip(self, x, y, z, core):
        return ((z % 2) * 8 + y * 2 + core, x, z // 2)

    def sibling(self):
        return self.chip(self.x, self.y, self.z, 1 - self.core)

    def along_z(self, d):
        return self.chip(self.x, self.y, (self.z + d) % 4, self.core)

    def flat(self, a, b):
        return self.chip((self.x + a) % 4, (self.y + b) % 4, self.z, self.core)

    def plane(self, n, a, b):
        if n == 1:
            return self.chip((self.x + a) % 4, self.y, (self.z + b) % 4, self.core)
        on, off = 1 - self.core, self.core
        x = (self.x + a * on) % 4
        y = (self.y + b * on + a * off) % 4
        z = (self.z + b * off) % 4
        return self.chip(x, y, z, self.core)

    def spot(self, n, a=0, b=0):
        if n == 1:
            return ((self.x + a) % 4) * 4 + (self.z + b) % 4
        first = jnp.where(self.core == 0, self.x, self.y)
        second = jnp.where(self.core == 0, self.y, self.z)
        return ((first + a) % 4) * 4 + (second + b) % 4

    def axis(self, n):
        return self.y if n == 1 else jnp.where(self.core == 0, self.z, self.x)

    def along(self, n, d):
        if n == 1:
            return self.flat(0, d)
        on, off = 1 - self.core, self.core
        return self.chip((self.x + d * off) % 4, self.y, (self.z + d * on) % 4, self.core)


def remote(src, dst, send, recv, device):
    return pltpu.make_async_remote_copy(
        src_ref=src,
        dst_ref=dst,
        send_sem=send,
        recv_sem=recv,
        device_id=device,
        device_id_type=MESH,
    )


def enter(place):
    lon, lat, ch = place.lon, place.lat, place.ch
    barrier = pltpu.get_barrier_semaphore()
    row = (lat + 2 * ch + 3) % 4
    devices = [(lon, lat, 1 - ch), (lon, row, 0), (lon, row, 1)]
    for side in (1, 15):
        for other in (0, 1):
            devices.append(((lon + side) % 16, lat, other))
            devices.append(((lon + side) % 16, row, other))
    devices.append(place.sibling())
    devices += [place.along_z(d) for d in (1, 2, 3)]
    devices += [place.flat(a, b) for a, b in OFFSETS]
    devices += [place.plane(1, a, b) for a, b in OFFSETS if a and b]
    for device in devices:
        pl.semaphore_signal(barrier, inc=1, device_id=device, device_id_type=MESH)

    @pl.when(place.core == 1)
    def _():
        for a, b in OFFSETS:
            if a and b:
                pl.semaphore_signal(
                    barrier, inc=1, device_id=place.plane(0, a, b), device_id_type=MESH
                )

    return barrier, len(devices) + 9 * place.core


def shuffle_latents(x_ref, own, rim_out):
    rows, cols = iota((512, 512), 0), iota((512, 512), 1)
    swap = onehot(cols == ((rows & 31) << 4) + (rows >> 5))
    b, n = iota((128, 256), 0), iota((128, 256), 1)
    parity = jnp.where(n < 64, 2 * n, 2 * n - 127)
    edge = jnp.where(n < 192, 0, 127)
    spread = onehot(b == jnp.where(n < 128, parity, edge))
    r, j = iota((512, 128), 0), iota((512, 128), 1)
    slot = (j & 63) - ((r & 15) << 2)
    rims = jnp.zeros((512, 128), F32)
    for pair in range(2):
        blocks = []
        for level in (2 * pair, 2 * pair + 1):
            block = mm(x_ref[level].reshape(512, 128), spread)
            rims = jnp.where(slot == level, block[:, 128:], rims)
            blocks.append(block[:, :128].astype(BF))
        moved = mm(swap, jnp.concatenate(blocks, axis=1)).astype(BF)
        own[2 * pair] = moved[:, :128].reshape(16, 32, 128)
        own[2 * pair + 1] = moved[:, 128:].reshape(16, 32, 128)
    c, k = iota((32, 512), 0), iota((32, 512), 1)
    rim_out[...] = mm(onehot((k >> 4) == c), rims.astype(BF)).astype(BF)


def pack_weights(cw_ref, gamma_ref, beta_ref, wl, gb):
    for k in range(13):
        wl[:, 128 * k : 128 * k + 128] = jnp.concatenate(
            [cw_ref[2 * k].astype(F32), cw_ref[2 * k + 1].astype(F32)], axis=1
        ).astype(BF)
    wl[:, 1664:1792] = jnp.concatenate(
        [cw_ref[26].astype(F32), jnp.zeros((32, 64), F32)], axis=1
    ).astype(BF)
    line = beta_ref[...].reshape(1, 32)
    column = jnp.sum(
        jnp.where(iota((32, 32), 0) == iota((32, 32), 1), line, 0.0), axis=1, keepdims=True
    )
    gb[:, 0:32] = gamma_ref[...]
    gb[:, 32:128] = jnp.broadcast_to(column, (32, 96))


def prepare_small(hw, hb_ref, pw, pb_ref, hwt, pwt, hbt, pbt):
    eye = onehot(iota((128, 128), 0) == iota((128, 128), 1))
    for k in range(5):
        part = slice(128 * k, 128 * k + 128)
        hwt[part, :] = mm(eye, hw[:, part], NT).astype(BF)
        hbt[part, :] = jnp.broadcast_to(hb_ref[part].reshape(1, 128), (128, 128)).T
    for k in range(2):
        part = slice(128 * k, 128 * k + 128)
        pwt[part, :] = mm(eye, pw[:, part], NT).astype(BF)
        pbt[part, :] = jnp.broadcast_to(pb_ref[part].reshape(1, 128), (128, 128)).T


def build_gamma(gall, gam, gamt, beta):
    k, n = iota((128, 256), 0), iota((128, 256), 1)
    copies = onehot(k == (n & 31))
    for g in range(2):
        high, low = split(gall[g])
        for which, part in ((0, high), (1, low)):
            wide = mm(part, copies)
            for s in range(4):
                block = g * 4 + s
                own_block = (iota((32, 256), 1) >> 5) == block
                gam[which, block * 32 : block * 32 + 32, :] = jnp.where(own_block, wide, 0.0)
        for s in range(4):
            block = g * 4 + s
            beta[block * 32 : block * 32 + 32, :] = jnp.broadcast_to(
                gall[g][:, 64:65], (32, 256)
            )
    for which in range(2):
        gamt[which] = gam[which].T


def build_weights(wall, wf):
    lane = iota((32, 256), 1)
    for g in range(2):
        for n in range(9):
            dl, da = n // 3, n % 3
            base = (192 * n) // 128 * 128
            v = wall[g, :, base : base + 256].astype(F32)
            first = v if n % 2 == 0 else pltpu.roll(v, 192, 1)
            second = v if n % 2 == 1 else pltpu.roll(v, 64, 1)
            first = jnp.where(lane < 192, first, 0.0).astype(BF)
            second = jnp.where(lane >= 64, second, 0.0).astype(BF)
            for p in range(2):
                r = da + p
                row = g * 128 + 2 * p * 32
                wf[dl, row : row + 32, 256 * r : 256 * r + 256] = first
                wf[dl, row + 32 : row + 64, 256 * r : 256 * r + 256] = second
        for dl in range(3):
            for p in range(2):
                r = 3 if p == 0 else 0
                row = g * 128 + 2 * p * 32
                wf[dl, row : row + 64, 256 * r : 256 * r + 256] = jnp.zeros((64, 256), BF)


def place_rims(place, rim_in, rims):
    chi, lat = place.ch, place.lat
    k, n = iota((512, 128), 0), iota((512, 128), 1)
    block, kk, nn = k >> 7, k & 127, n & 63
    left = block < 2
    same = (block & 1) == 0
    pole = jnp.where(chi == 0, lat, 3 - lat) == 0
    shift_same = (8 * chi - 1) * 4
    other_low = 36 * chi
    shift_other = jnp.where(chi == 0, 60, -36)
    shift = jnp.where(same, shift_same, shift_other)
    source = nn + shift
    inside = (source >= 0) & (source < 64) & (nn < 40)
    only = (nn >= other_low) & (nn < other_low + 4) & jnp.logical_not(pole)
    valid = inside & (same | only)
    side = (left & (n < 64)) | (jnp.logical_not(left) & (n >= 64))
    chosen = kk == source + jnp.where(left, 64, 0)
    pick = onehot(valid & side & chosen)
    tiles = jnp.concatenate(
        [rim_in[s, t].reshape(64, 128) for s in range(2) for t in range(2)], axis=1
    )
    rims[...] = mm(tiles, pick)


def window_pick():
    col = iota((1, 512), 1)
    w, js, m = col >> 7, (col & 127) >> 6, col & 63
    target = jnp.where(
        w == 0,
        jnp.where(m == 0, 256 + js * 8, js * 128 + 63 + m),
        jnp.where(
            w == 1,
            js * 128 + m,
            jnp.where(
                w == 2,
                js * 128 + 64 + m,
                jnp.where(m == 63, 320 + js * 8, js * 128 + m + 1),
            ),
        ),
    )
    return onehot(iota((384, 512), 0) == target)


def build_windows(field, rims, pick, xt, level):
    stack = []
    for r in range(4):
        for pair in range(2):
            j0 = r + 4 * pair
            edge = pltpu.roll(rims[...], 128 - (j0 * 4 + level), 1).astype(BF)
            rows = [field[level, :, j].reshape(64, 128) for j in (j0, j0 + 2)]
            stack.append(jnp.concatenate(rows + [edge], axis=1))
    out = mm(jnp.concatenate(stack, axis=0), pick[...]).astype(BF)
    for r in range(4):
        for pair in range(2):
            row, lane = (r * 2 + pair) * 64, level * 256 + pair * 128
            for v in range(4):
                xt[r * 256 + v * 64 : r * 256 + v * 64 + 64, lane : lane + 128] = out[
                    row : row + 64, v * 128 : v * 128 + 128
                ]


def mix(gam, value):
    high, low = split(value)
    ghigh, glow = gam[0].astype(BF), gam[1].astype(BF)
    return mm(ghigh, high) + (mm(ghigh, low) + mm(glow, high))


def forward(s, level):
    lanes = slice(256 * level, 256 * level + 256)
    total = None
    for dl in range(3):
        other = level + dl - 1
        if 0 <= other < 4:
            term = mm(s["wf"][dl], s["xt"][:, 256 * other : 256 * other + 256])
            total = term if total is None else total + term
    s["conv"][:, lanes] = total
    inv = lax.rsqrt(s["beta"][...] + mix(s["gam"], total * total))
    s["inv"][:, lanes] = inv
    s["normed"][:, lanes] = (total * inv).astype(BF)


def entropy_forward(s):
    def first(i, carry):
        lanes = pl.ds(pl.multiple_of(i * 256, 256), 256)
        features = s["normed"][0:128, lanes]
        for k in range(5):
            part = slice(128 * k, 128 * k + 128)
            bias = s["hbt"][part, :]
            pre = mm(s["hwt"][part, :], features) + jnp.concatenate([bias, bias], axis=1)
            sig = 0.5 * jnp.tanh(0.5 * pre) + 0.5
            act = pre * sig
            s["hidden"][part, lanes] = act.astype(BF)
            s["gate"][part, lanes] = sig * (1.0 + pre - act)
        return carry

    lax.fori_loop(0, 4, first, 0)

    def second(i, carry):
        lanes = pl.ds(pl.multiple_of(i * 256, 256), 256)
        hidden = s["hidden"][:, lanes]
        cb, rb = s["pbt"][0:128, :], s["pbt"][128:256, :]
        centre = mm(s["pwt"][0:128, :], hidden) + jnp.concatenate([cb, cb], axis=1)
        raw = mm(s["pwt"][128:256, :], hidden) + jnp.concatenate([rb, rb], axis=1)
        small = jnp.exp(-jnp.abs(raw))
        spread = 0.5 + jnp.maximum(raw, 0.0) + jnp.log(1.0 + small)
        fraction = 1.0 / (1.0 + small)
        sig = jnp.where(raw >= 0.0, fraction, small * fraction)
        over = 1.0 / spread
        error = (s["normed"][128:256, lanes].astype(F32) - centre) * over
        ratio = error * over * (1.0 / PATCHES)
        s["dparams"][0:128, lanes] = (-ratio).astype(BF)
        s["dparams"][128:256, lanes] = (
            (1.0 - error * error) * over * sig * (1.0 / PATCHES)
        ).astype(BF)
        s["dtargets"][:, lanes] = ratio.astype(BF)
        return carry

    lax.fori_loop(0, 4, second, 0)

    grad = mm(s["hidden"][...], s["dparams"][...], NT)
    for half in range(2):
        s["ppart"][half] = grad[:, 128 * half : 128 * half + 128].reshape(16, 40, 128)


def entropy_backward(s, pw):
    def third(i, carry):
        lanes = pl.ds(pl.multiple_of(i * 256, 256), 256)
        back = mm(pw[...], s["dparams"][:, lanes])
        s["dpre"][:, lanes] = (back * s["gate"][:, lanes]).astype(BF)
        return carry

    lax.fori_loop(0, 4, third, 0)


def hidden_grads(s):
    hpart = s["hpart"]
    ones = jnp.ones((8, 1024), BF)
    pb = mm(ones, s["dparams"][...], NT)
    grad = mm(s["normed"][0:128, :], s["dpre"][...], NT)
    hb = mm(ones, s["dpre"][...], NT)
    zeros = jnp.zeros((1, 128), F32)
    lines = [hb[0:1, 128 * k : 128 * k + 128] for k in range(5)]
    lines += [pb[0:1, 0:128], pb[0:1, 128:256], zeros]
    for t in range(80):
        core, place, row = tile_spot(t)
        n, k = t // 5, t % 5
        hpart[core, place, row : row + 8] = grad[8 * n : 8 * n + 8, 128 * k : 128 * k + 128]
    hpart[0, 13, 8:16] = jnp.concatenate(lines, axis=0)
    hpart[1, 13, 8:16] = jnp.zeros((8, 128), F32)
    for core in range(2):
        hpart[core, 13, 16:24] = jnp.zeros((8, 128), F32)
        hpart[core, 14:16] = jnp.zeros((2, 24, 128), F32)


def conv_backward(s, hw):
    for level in range(4):
        lanes = slice(256 * level, 256 * level + 256)
        dfeat = mm(hw[...], s["dpre"][:, lanes]).astype(BF).astype(F32)
        dn = jnp.concatenate([dfeat, s["dtargets"][:, lanes].astype(F32)], axis=0)
        inv = s["inv"][:, lanes]
        y = s["conv"][:, lanes]
        dni = dn * inv
        weighted = dni * y * (inv * inv)
        s["dconv"][:, lanes] = (dni - y * mix(s["gamt"], weighted)).astype(BF)


def weight_grads(s):
    for dl in range(3):
        first, last = max(0, 1 - dl), min(4, 5 - dl)
        d = s["dconv"][:, 256 * first : 256 * last]
        x = s["xt"][:, 256 * (first + dl - 1) : 256 * (last + dl - 1)]
        s["taps"][dl] = mm(d, x, NT)
    for dl in range(3):
        for da in range(3):
            n = dl * 3 + da
            for g in range(2):
                total = None
                for p in range(2):
                    row = g * 128 + 2 * p * 32
                    lanes = slice(256 * (da + p), 256 * (da + p) + 256)
                    a = s["taps"][dl, row : row + 32, lanes]
                    b = s["taps"][dl, row + 32 : row + 64, lanes]
                    term = a + pltpu.roll(b, 192, 1)
                    total = term if total is None else total + term
                s["wgrad"][32 * g : 32 * g + 32, 192 * n : 192 * n + 192] = total[:, 0:192]
    s["wgrad"][:, 1728:2048] = jnp.zeros((64, 320), F32)
    lane = iota((8, 128), 1) >> 5
    for k in range(64):
        first = 27 * k
        base = first // 128 * 128
        offset = first - base
        wide = 128 if offset <= 101 else 256
        lon, x = k // 4, k % 4
        core, y, zlo = lon % 2, (lon // 2) % 4, lon // 8
        for g in range(2):
            tile = None
            for q in range(4):
                v = s["wgrad"][32 * g + 8 * q : 32 * g + 8 * q + 8, base : base + wide]
                shift = (32 * q - offset) % wide
                v = pltpu.roll(v, shift, 1)[:, 0:128] if shift else v[:, 0:128]
                tile = v if tile is None else jnp.where(lane == q, v, tile)
            s["cpart"][core, g * 2 + zlo, y, x] = tile


def body(
    x_hbm, cw_hbm, gamma_ref, beta_ref, hw_hbm, hb_ref, pw_hbm, pb_ref,
    ptotal, htotal, cg_ref,
    x, cw, hw, pw, wl, gb,
    own, rim_out, rim_in, field, wall, gall, rims, pick,
    xt, wf, gam, gamt, beta, hwt, pwt, hbt, pbt,
    conv, inv, normed, hidden, gate, dparams, dtargets, dpre, dconv, taps, wgrad,
    ppart, hpart, cpart, pr1, hr1, pr2, hr2, pr3, hr3, q1, q2, q3,
    local_sem, xs, xr, ks, kr, bs, br, es, er, gs, gr, cs, cr,
):
    place = Place()
    lon, lat, chi = place.lon, place.lat, place.ch
    core, z, y = place.core, place.z, place.y
    partner = (lon, lat, 1 - chi)
    sibling = place.sibling()
    other = 1 - chi
    loads = [
        pltpu.make_async_copy(src, dst, local_sem.at[n])
        for n, (src, dst) in enumerate(((x_hbm, x), (cw_hbm, cw), (hw_hbm, hw), (pw_hbm, pw)))
    ]
    for copy in loads:
        copy.start()
    barrier, count = enter(place)
    loads[1].wait()
    pack_weights(cw, gamma_ref, beta_ref, wl, gb)
    loads[0].wait()
    shuffle_latents(x, own, rim_out)
    pl.semaphore_wait(barrier, count)

    mine = pl.ds(pl.multiple_of(16 * core, 16), 16)
    theirs = pl.ds(pl.multiple_of(16 * (1 - core), 16), 16)
    sends = []

    def start(*copies):
        for copy in copies:
            copy.start()
        sends.extend(copies)
        return copies

    def arrive(copies):
        for copy in copies:
            copy.wait_recv()

    start(
        remote(wl.at[mine], wall.at[chi, mine], xs.at[4], xr.at[4], partner),
        remote(gb, gall.at[chi], xs.at[5], xr.at[5], partner),
    )
    down, up = (lat + 3) % 4, (lat + 1) % 4
    for side in range(2):
        near = (lon + 1) % 16 if side == 0 else (lon + 15) % 16
        for kind, (row, half) in enumerate(((lat, 0), (lat, 1), (down, 1), (up, 0))):
            slot = 9 + (side * 2 + kind // 2) * 2
            start(
                remote(
                    rim_out, rim_in.at[side, kind // 2, chi],
                    xs.at[9 + side * 4 + kind], xr.at[slot + chi], (near, row, half),
                )
            )
    start(
        remote(own.at[:, 0], field.at[:, chi, 9], xs.at[7], xr.at[7 + chi], (lon, down, 1)),
        remote(own.at[:, 15], field.at[:, chi, 0], xs.at[8], xr.at[7 + chi], (lon, up, 0)),
    )
    levels = [
        remote(
            own.at[level, pl.ds(7 * other, 9)], field.at[level, chi, pl.ds(chi, 9)],
            xs.at[level], xr.at[level], partner,
        )
        for level in range(4)
    ]
    levels[0].start()
    levels[1].start()
    for level in range(4):
        field[level, chi, pl.ds(other, 9)] = own[level, pl.ds(7 * chi, 9)]
    wall[chi] = wl[...]
    gall[chi] = gb[...]
    loads[2].wait()
    loads[3].wait()
    prepare_small(hw, hb_ref, pw, pb_ref, hwt, pwt, hbt, pbt)
    pick[...] = window_pick()
    remote(gb, gall.at[other], xs.at[5], xr.at[5], partner).wait_recv()
    remote(wl.at[mine], wall.at[other, mine], xs.at[4], xr.at[4], partner).wait_recv()
    start(remote(wall.at[other, mine], wall.at[other, mine], xs.at[6], xr.at[6], sibling))
    levels[0].wait_send()
    levels[2].start()
    build_gamma(gall, gam, gamt, beta)
    levels[1].wait_send()
    levels[3].start()
    for half in range(2):
        remote(
            own.at[:, 0], field.at[:, half, 9 * chi], xs.at[7], xr.at[7 + half], partner
        ).wait_recv()
    for side in range(2):
        for kind in range(2):
            for half in range(2):
                remote(
                    rim_out, rim_in.at[side, kind, half], xs.at[9],
                    xr.at[9 + (side * 2 + kind) * 2 + half], partner,
                ).wait_recv()
    place_rims(place, rim_in, rims)
    remote(
        wall.at[other, mine], wall.at[other, theirs], xs.at[6], xr.at[6], sibling
    ).wait_recv()
    build_weights(wall, wf)

    @pl.when(jnp.where(chi == 0, lat, 3 - lat) == 0)
    def _():
        field[:, :, pl.ds(9 * chi, 1)] = jnp.zeros((4, 2, 1, 32, 128), BF)

    s = {
        "xt": xt, "wf": wf, "gam": gam, "gamt": gamt, "beta": beta, "hwt": hwt, "pwt": pwt,
        "hbt": hbt, "pbt": pbt, "conv": conv, "inv": inv, "normed": normed, "hidden": hidden,
        "gate": gate, "dparams": dparams, "dtargets": dtargets, "dpre": dpre, "dconv": dconv,
        "taps": taps, "wgrad": wgrad, "ppart": ppart, "hpart": hpart, "cpart": cpart,
    }
    for level in range(4):
        remote(
            own.at[level, pl.ds(0, 9)], field.at[level, other, pl.ds(other, 9)],
            xs.at[level], xr.at[level], partner,
        ).wait_recv()
        build_windows(field, rims, pick, xt, level)
        if level >= 1:
            forward(s, level - 1)
    sends.extend(levels[2:])
    forward(s, 3)
    entropy_forward(s)

    parts, totals = (ppart, hpart), (ptotal, htotal)
    firsts, seconds, thirds = (pr1, hr1), (pr2, hr2), (pr3, hr3)

    def core_stage(n):
        return start(
            remote(parts[n].at[1 - core], firsts[n], ks.at[n], kr.at[n], sibling)
        )

    def core_add(n):
        parts[n][core] = parts[n][core] + firsts[n][...]

    def plane_stage(n):
        return start(
            *[
                remote(
                    parts[n].at[core, place.spot(n, a, b)], seconds[n].at[4 * a + b],
                    bs.at[n, 4 * a + b], br.at[n, 4 * a + b], place.plane(n, a, b),
                )
                for a, b in OFFSETS
            ]
        )

    def plane_add(n):
        terms = [parts[n][core, place.spot(n)]] + [seconds[n][k] for k in range(1, 16)]
        while len(terms) > 1:
            terms = [terms[k] + terms[k + 1] for k in range(0, len(terms), 2)]
        thirds[n][place.axis(n)] = terms[0]

    def axis_stage(n):
        axis = place.axis(n)
        copies = start(
            *[
                remote(
                    thirds[n].at[axis], thirds[n].at[axis],
                    es.at[n, d], er.at[n, d], place.along(n, d),
                )
                for d in (1, 2, 3)
            ]
        )
        return [
            remote(
                thirds[n].at[axis], thirds[n].at[(axis + 4 - d) % 4],
                es.at[n, d], er.at[n, d], sibling,
            )
            for d in (1, 2, 3)
        ]

    def axis_add(n):
        totals[n][core, place.spot(n)] = (thirds[n][0] + thirds[n][1]) + (thirds[n][2] + thirds[n][3])

    def spread_stage(n):
        view = totals[n].at[core, place.spot(n)]
        start(
            *[
                remote(
                    view, view, gs.at[n, 4 * a + b], gr.at[n, 4 * a + b], place.plane(n, a, b)
                )
                for a, b in OFFSETS
            ]
        )
        return [
            remote(
                view, totals[n].at[core, place.spot(n, 4 - a, 4 - b)],
                gs.at[n, 4 * a + b], gr.at[n, 4 * a + b], sibling,
            )
            for a, b in OFFSETS
        ]

    def core_spread(n):
        view = totals[n].at[core]
        start(remote(view, view, ks.at[2 + n], kr.at[2 + n], sibling))
        return [remote(view, totals[n].at[1 - core], ks.at[2 + n], kr.at[2 + n], sibling)]

    core_p = core_stage(0)
    entropy_backward(s, pw)
    arrive(core_p)
    core_add(0)
    plane_p = plane_stage(0)
    hidden_grads(s)
    core_h = core_stage(1)
    conv_backward(s, hw)
    arrive(core_h)
    core_add(1)
    plane_h = plane_stage(1)
    weight_grads(s)
    core_c = start(remote(cpart.at[1 - core], q1, cs.at[0], cr.at[0], sibling))
    arrive(core_c)
    cpart[core] = cpart[core] + q1[...]
    axis_c = start(
        *[
            remote(
                cpart.at[core, (z + d) % 4], q2.at[d - 1], cs.at[d], cr.at[d], place.along_z(d)
            )
            for d in (1, 2, 3)
        ]
    )
    arrive(plane_p)
    plane_add(0)
    axis_p = axis_stage(0)
    arrive(plane_h)
    plane_add(1)
    axis_h = axis_stage(1)
    arrive(axis_c)
    cpart[core, z] = (cpart[core, z] + q2[0]) + (q2[1] + q2[2])
    plane_c = start(
        *[
            remote(
                cpart.at[core, z, (y + b) % 4, (place.x + a) % 4], q3.at[4 * a + b],
                cs.at[3 + 4 * a + b],
                cr.at[3 + 4 * a + b], place.flat(a, b),
            )
            for a, b in OFFSETS
        ]
    )
    arrive(axis_p)
    axis_add(0)
    spread_p = spread_stage(0)
    arrive(axis_h)
    axis_add(1)
    spread_h = spread_stage(1)
    arrive(plane_c)
    terms = [cpart[core, z, y, place.x]] + [q3[k] for k in range(1, 16)]
    while len(terms) > 1:
        terms = [terms[k] + terms[k + 1] for k in range(0, len(terms), 2)]
    for q in range(4):
        v = pltpu.roll(terms[0], 128 - 32 * q, 1) if q else terms[0]
        cg_ref[8 * q : 8 * q + 8, :] = v
    arrive(spread_p)
    core_p = core_spread(0)
    arrive(spread_h)
    core_h = core_spread(1)
    arrive(core_p)
    arrive(core_h)
    for copy in sends:
        copy.wait_send()


def unpack(ptotal, htotal, block_ref, cg_ref, hwg_ref, hbg_ref, pwg_ref, pbg_ref):
    cg_ref[...] = block_ref[:, 0:27]
    for half in range(2):
        pwg_ref[:, 128 * half : 128 * half + 128] = ptotal[half].reshape(640, 128)
    for t in range(80):
        core, place, row = tile_spot(t)
        n, k = t // 5, t % 5
        hwg_ref[8 * n : 8 * n + 8, 128 * k : 128 * k + 128] = htotal[core, place, row : row + 8]
    for k in range(5):
        hbg_ref[128 * k : 128 * k + 128] = htotal[0, 13, 8 + k]
    for k in range(2):
        pbg_ref[128 * k : 128 * k + 128] = htotal[0, 13, 13 + k]


def on_device(x, cw, gamma, beta, hw, hb, pw, pb):
    vmem = pltpu.VMEM
    dma = pltpu.SemaphoreType.DMA
    scratch = [
        vmem((4, 32, 16, 128), BF),
        vmem((27, 32, 64), BF),
        vmem((128, 640), BF),
        vmem((640, 256), BF),
        vmem((32, 1792), BF),
        vmem((32, 128), F32),
        vmem((4, 16, 32, 128), BF),
        vmem((32, 128), BF),
        vmem((2, 2, 2, 32, 128), BF),
        vmem((4, 2, 10, 32, 128), BF),
        vmem((2, 32, 1792), BF),
        vmem((2, 32, 128), F32),
        vmem((64, 128), F32),
        vmem((384, 512), BF),
        vmem((1024, 1024), BF),
        vmem((3, 256, 1024), BF),
        vmem((2, 256, 256), F32),
        vmem((2, 256, 256), F32),
        vmem((256, 256), F32),
        vmem((640, 128), BF),
        vmem((256, 640), BF),
        vmem((640, 128), F32),
        vmem((256, 128), F32),
        vmem((256, 1024), F32),
        vmem((256, 1024), F32),
        vmem((256, 1024), BF),
        vmem((640, 1024), BF),
        vmem((640, 1024), F32),
        vmem((256, 1024), BF),
        vmem((128, 1024), BF),
        vmem((640, 1024), BF),
        vmem((256, 1024), BF),
        vmem((3, 256, 1024), F32),
        vmem((64, 2048), F32),
        vmem((2, 16, 40, 128), F32),
        vmem((2, 16, 24, 128), F32),
        vmem((2, 4, 4, 4, 8, 128), F32),
        vmem((16, 40, 128), F32),
        vmem((16, 24, 128), F32),
        vmem((16, 40, 128), F32),
        vmem((16, 24, 128), F32),
        vmem((4, 40, 128), F32),
        vmem((4, 24, 128), F32),
        vmem((4, 4, 4, 8, 128), F32),
        vmem((3, 4, 4, 8, 128), F32),
        vmem((16, 8, 128), F32),
        dma((4,)),
        dma((17,)),
        dma((17,)),
        dma((4,)),
        dma((4,)),
        dma((2, 16)),
        dma((2, 16)),
        dma((2, 4)),
        dma((2, 4)),
        dma((2, 16)),
        dma((2, 16)),
        dma((19,)),
        dma((19,)),
    ]
    spec = pl.BlockSpec(memory_space=pltpu.VMEM)
    anywhere = pl.BlockSpec(memory_space=pl.ANY)
    ptotal, htotal, block = pl.pallas_call(
        body,
        out_shape=(
            jax.ShapeDtypeStruct((2, 16, 40, 128), F32),
            jax.ShapeDtypeStruct((2, 16, 24, 128), F32),
            jax.ShapeDtypeStruct((32, 128), F32),
        ),
        in_specs=[anywhere, anywhere, spec, spec, anywhere, spec, anywhere, spec],
        out_specs=(spec, spec, spec),
        scratch_shapes=scratch,
        compiler_params=pltpu.CompilerParams(
            collective_id=0, has_side_effects=True, vmem_limit_bytes=56 * 1024 * 1024
        ),
    )(x, jnp.transpose(cw, (1, 0, 2)), gamma, beta, hw, hb, pw, pb)
    return pl.pallas_call(
        unpack,
        out_shape=(
            jax.ShapeDtypeStruct((32, 27), F32),
            jax.ShapeDtypeStruct((128, 640), F32),
            jax.ShapeDtypeStruct((640,), F32),
            jax.ShapeDtypeStruct((640, 256), F32),
            jax.ShapeDtypeStruct((256,), F32),
        ),
        in_specs=[spec] * 3,
        out_specs=(spec,) * 5,
    )(ptotal, htotal, block)


def solution(mesh):
    placed = (
        P(None, "ch", "lat", "lon"),
        P("ch", None, None),
        P("ch", None),
        P("ch"),
        P(),
        P(),
        P(),
        P(),
    )
    return jax.shard_map(
        on_device,
        mesh=mesh,
        in_specs=placed,
        out_specs=(P("ch", ("lon", "lat")), P(), P(), P(), P()),
        check_vma=False,
    )
```

```python
import jax
import jax.numpy as jnp
from jax import lax
from jax.experimental import pallas as pl
from jax.experimental.pallas import tpu as pltpu
from jax.sharding import PartitionSpec as P

BF = jnp.bfloat16
F32 = jnp.float32
MESH = pl.DeviceIdType.MESH
PATCHES = 131072.0
OFFSETS = [(a, b) for a in range(4) for b in range(4) if a or b]

NN = (((1,), (0,)), ((), ()))
NT = (((1,), (1,)), ((), ()))


def mm(a, b, dims=NN):
    return lax.dot_general(a, b, dims, preferred_element_type=F32)


def iota(shape, dim):
    return lax.broadcasted_iota(jnp.int32, shape, dim)


def onehot(condition):
    return jnp.where(condition, 1.0, 0.0).astype(BF)


def tile_spot(t):
    core, rest = divmod(t, 40)
    return core, rest // 3, 8 * (rest % 3)


def split(value):
    high = value.astype(BF)
    return high, (value - high.astype(F32)).astype(BF)


class Place:
    def __init__(self):
        self.lon = lax.axis_index("lon")
        self.lat = lax.axis_index("lat")
        self.ch = lax.axis_index("ch")
        self.core = self.lon % 2
        self.y = (self.lon // 2) % 4
        self.zlo = self.lon // 8
        self.x = self.lat
        self.z = self.ch * 2 + self.zlo

    def chip(self, x, y, z, core):
        return ((z % 2) * 8 + y * 2 + core, x, z // 2)

    def sibling(self):
        return self.chip(self.x, self.y, self.z, 1 - self.core)

    def along_z(self, d):
        return self.chip(self.x, self.y, (self.z + d) % 4, self.core)

    def flat(self, a, b):
        return self.chip((self.x + a) % 4, (self.y + b) % 4, self.z, self.core)

    def plane(self, n, a, b):
        if n == 1:
            return self.chip((self.x + a) % 4, self.y, (self.z + b) % 4, self.core)
        on, off = 1 - self.core, self.core
        x = (self.x + a * on) % 4
        y = (self.y + b * on + a * off) % 4
        z = (self.z + b * off) % 4
        return self.chip(x, y, z, self.core)

    def spot(self, n, a=0, b=0):
        if n == 1:
            return ((self.x + a) % 4) * 4 + (self.z + b) % 4
        first = jnp.where(self.core == 0, self.x, self.y)
        second = jnp.where(self.core == 0, self.y, self.z)
        return ((first + a) % 4) * 4 + (second + b) % 4

    def axis(self, n):
        return self.y if n == 1 else jnp.where(self.core == 0, self.z, self.x)

    def along(self, n, d):
        if n == 1:
            return self.flat(0, d)
        on, off = 1 - self.core, self.core
        return self.chip((self.x + d * off) % 4, self.y, (self.z + d * on) % 4, self.core)


def remote(src, dst, send, recv, device):
    return pltpu.make_async_remote_copy(
        src_ref=src,
        dst_ref=dst,
        send_sem=send,
        recv_sem=recv,
        device_id=device,
        device_id_type=MESH,
    )


def enter(place):
    lon, lat, ch = place.lon, place.lat, place.ch
    barrier = pltpu.get_barrier_semaphore()
    row = (lat + 2 * ch + 3) % 4
    devices = [(lon, lat, 1 - ch), (lon, row, 0), (lon, row, 1)]
    for side in (1, 15):
        for other in (0, 1):
            devices.append(((lon + side) % 16, lat, other))
            devices.append(((lon + side) % 16, row, other))
    devices.append(place.sibling())
    devices += [place.along_z(d) for d in (1, 2, 3)]
    devices += [place.flat(a, b) for a, b in OFFSETS]
    devices += [place.plane(1, a, b) for a, b in OFFSETS if a and b]
    for device in devices:
        pl.semaphore_signal(barrier, inc=1, device_id=device, device_id_type=MESH)

    @pl.when(place.core == 1)
    def _():
        for a, b in OFFSETS:
            if a and b:
                pl.semaphore_signal(
                    barrier, inc=1, device_id=place.plane(0, a, b), device_id_type=MESH
                )

    return barrier, len(devices) + 9 * place.core


def shuffle_latents(x_ref, own, rim_out):
    rows, cols = iota((512, 512), 0), iota((512, 512), 1)
    swap = onehot(cols == ((rows & 31) << 4) + (rows >> 5))
    b, n = iota((128, 256), 0), iota((128, 256), 1)
    parity = jnp.where(n < 64, 2 * n, 2 * n - 127)
    edge = jnp.where(n < 192, 0, 127)
    spread = onehot(b == jnp.where(n < 128, parity, edge))
    r, j = iota((512, 128), 0), iota((512, 128), 1)
    slot = (j & 63) - ((r & 15) << 2)
    rims = jnp.zeros((512, 128), F32)
    for pair in range(2):
        blocks = []
        for level in (2 * pair, 2 * pair + 1):
            block = mm(x_ref[level].reshape(512, 128), spread)
            rims = jnp.where(slot == level, block[:, 128:], rims)
            blocks.append(block[:, :128].astype(BF))
        moved = mm(swap, jnp.concatenate(blocks, axis=1)).astype(BF)
        own[2 * pair] = moved[:, :128].reshape(16, 32, 128)
        own[2 * pair + 1] = moved[:, 128:].reshape(16, 32, 128)
    c, k = iota((32, 512), 0), iota((32, 512), 1)
    rim_out[...] = mm(onehot((k >> 4) == c), rims.astype(BF)).astype(BF)


def pack_weights(cw_ref, gamma_ref, beta_ref, wl, gb):
    for k in range(13):
        wl[:, 128 * k : 128 * k + 128] = jnp.concatenate(
            [cw_ref[2 * k].astype(F32), cw_ref[2 * k + 1].astype(F32)], axis=1
        ).astype(BF)
    wl[:, 1664:1792] = jnp.concatenate(
        [cw_ref[26].astype(F32), jnp.zeros((32, 64), F32)], axis=1
    ).astype(BF)
    line = beta_ref[...].reshape(1, 32)
    column = jnp.sum(
        jnp.where(iota((32, 32), 0) == iota((32, 32), 1), line, 0.0), axis=1, keepdims=True
    )
    gb[:, 0:32] = gamma_ref[...]
    gb[:, 32:128] = jnp.broadcast_to(column, (32, 96))


def prepare_small(hw, hb_ref, pw, pb_ref, hwt, pwt, hbt, pbt):
    eye = onehot(iota((128, 128), 0) == iota((128, 128), 1))
    for k in range(5):
        part = slice(128 * k, 128 * k + 128)
        hwt[part, :] = mm(eye, hw[:, part], NT).astype(BF)
        hbt[part, :] = jnp.broadcast_to(hb_ref[part].reshape(1, 128), (128, 128)).T
    for k in range(2):
        part = slice(128 * k, 128 * k + 128)
        pwt[part, :] = mm(eye, pw[:, part], NT).astype(BF)
        pbt[part, :] = jnp.broadcast_to(pb_ref[part].reshape(1, 128), (128, 128)).T


def build_gamma(gall, gam, gamt, beta):
    k, n = iota((128, 256), 0), iota((128, 256), 1)
    copies = onehot(k == (n & 31))
    for g in range(2):
        for which, part in enumerate(split(gall[g])):
            wide = mm(part, copies)
            for block in range(4 * g, 4 * g + 4):
                own_block = (iota((32, 256), 1) >> 5) == block
                row = 256 * which + 32 * block
                gam[row : row + 32, :] = jnp.where(own_block, wide, 0.0).astype(BF)
        for block in range(4 * g, 4 * g + 4):
            beta[block * 32 : block * 32 + 32, :] = jnp.broadcast_to(
                gall[g][:, 64:65], (32, 256)
            )
    for which in range(2):
        part = slice(256 * which, 256 * which + 256)
        gamt[part, :] = gam[part, :].astype(F32).T.astype(BF)


def build_weights(wall, wf):
    lane = iota((32, 256), 1)
    for g in range(2):
        for n in range(9):
            dl, da = n // 3, n % 3
            base = (192 * n) // 128 * 128
            v = wall[g, :, base : base + 256].astype(F32)
            first = v if n % 2 == 0 else pltpu.roll(v, 192, 1)
            second = v if n % 2 == 1 else pltpu.roll(v, 64, 1)
            first = jnp.where(lane < 192, first, 0.0).astype(BF)
            second = jnp.where(lane >= 64, second, 0.0).astype(BF)
            for p in range(2):
                r = da + p
                row = g * 128 + 2 * p * 32
                wf[dl, row : row + 32, 256 * r : 256 * r + 256] = first
                wf[dl, row + 32 : row + 64, 256 * r : 256 * r + 256] = second
        for dl in range(3):
            for p in range(2):
                r = 3 if p == 0 else 0
                row = g * 128 + 2 * p * 32
                wf[dl, row : row + 64, 256 * r : 256 * r + 256] = jnp.zeros((64, 256), BF)


def place_rims(place, rim_in, rims):
    chi, lat = place.ch, place.lat
    k, n = iota((512, 128), 0), iota((512, 128), 1)
    block, kk, nn = k >> 7, k & 127, n & 63
    left = block < 2
    same = (block & 1) == 0
    pole = jnp.where(chi == 0, lat, 3 - lat) == 0
    shift_same = (8 * chi - 1) * 4
    other_low = 36 * chi
    shift_other = jnp.where(chi == 0, 60, -36)
    shift = jnp.where(same, shift_same, shift_other)
    source = nn + shift
    inside = (source >= 0) & (source < 64) & (nn < 40)
    only = (nn >= other_low) & (nn < other_low + 4) & jnp.logical_not(pole)
    valid = inside & (same | only)
    side = (left & (n < 64)) | (jnp.logical_not(left) & (n >= 64))
    chosen = kk == source + jnp.where(left, 64, 0)
    pick = onehot(valid & side & chosen)
    tiles = jnp.concatenate(
        [rim_in[s, t].reshape(64, 128) for s in range(2) for t in range(2)], axis=1
    )
    rims[...] = mm(tiles, pick)


def window_pick():
    col = iota((1, 512), 1)
    w, js, m = col >> 7, (col & 127) >> 6, col & 63
    target = jnp.where(
        w == 0,
        jnp.where(m == 0, 256 + js * 8, js * 128 + 63 + m),
        jnp.where(
            w == 1,
            js * 128 + m,
            jnp.where(
                w == 2,
                js * 128 + 64 + m,
                jnp.where(m == 63, 320 + js * 8, js * 128 + m + 1),
            ),
        ),
    )
    return onehot(iota((384, 512), 0) == target)


def build_windows(field, rims, pick, xt, level):
    stack = []
    for r in range(4):
        for pair in range(2):
            j0 = r + 4 * pair
            edge = pltpu.roll(rims[...], 128 - (j0 * 4 + level), 1).astype(BF)
            rows = [field[level, :, j].reshape(64, 128) for j in (j0, j0 + 2)]
            stack.append(jnp.concatenate(rows + [edge], axis=1))
    out = mm(jnp.concatenate(stack, axis=0), pick[...]).astype(BF)
    for r in range(4):
        for pair in range(2):
            row, lane = (r * 2 + pair) * 64, level * 256 + pair * 128
            for v in range(4):
                xt[r * 256 + v * 64 : r * 256 + v * 64 + 64, lane : lane + 128] = out[
                    row : row + 64, v * 128 : v * 128 + 128
                ]


def mix(gam, value):
    high, low = split(value)
    both = mm(gam[...], high)
    return both[0:256, :] + (both[256:512, :] + mm(gam[0:256, :], low))


def forward(s, level):
    lanes = slice(256 * level, 256 * level + 256)
    total = None
    for dl in range(3):
        other = level + dl - 1
        if 0 <= other < 4:
            term = mm(s["wf"][dl], s["xt"][:, 256 * other : 256 * other + 256])
            total = term if total is None else total + term
    s["conv"][:, lanes] = total
    inv = lax.rsqrt(s["beta"][...] + mix(s["gam"], total * total))
    s["inv"][:, lanes] = inv
    s["normed"][:, lanes] = (total * inv).astype(BF)


def entropy_forward(s):
    def first(i, carry):
        lanes = pl.ds(pl.multiple_of(i * 256, 256), 256)
        features = s["normed"][0:128, lanes]
        for k in range(5):
            part = slice(128 * k, 128 * k + 128)
            bias = s["hbt"][part, :]
            pre = mm(s["hwt"][part, :], features) + jnp.concatenate([bias, bias], axis=1)
            sig = 0.5 * jnp.tanh(0.5 * pre) + 0.5
            act = pre * sig
            s["hidden"][part, lanes] = act.astype(BF)
            s["gate"][part, lanes] = sig * (1.0 + pre - act)
        return carry

    lax.fori_loop(0, 4, first, 0)

    def second(i, carry):
        lanes = pl.ds(pl.multiple_of(i * 256, 256), 256)
        hidden = s["hidden"][:, lanes]
        cb, rb = s["pbt"][0:128, :], s["pbt"][128:256, :]
        centre = mm(s["pwt"][0:128, :], hidden) + jnp.concatenate([cb, cb], axis=1)
        raw = mm(s["pwt"][128:256, :], hidden) + jnp.concatenate([rb, rb], axis=1)
        small = jnp.exp(-jnp.abs(raw))
        spread = 0.5 + jnp.maximum(raw, 0.0) + jnp.log(1.0 + small)
        fraction = 1.0 / (1.0 + small)
        sig = jnp.where(raw >= 0.0, fraction, small * fraction)
        over = 1.0 / spread
        error = (s["normed"][128:256, lanes].astype(F32) - centre) * over
        ratio = error * over * (1.0 / PATCHES)
        s["dparams"][0:128, lanes] = (-ratio).astype(BF)
        s["dparams"][128:256, lanes] = (
            (1.0 - error * error) * over * sig * (1.0 / PATCHES)
        ).astype(BF)
        s["dtargets"][:, lanes] = ratio.astype(BF)
        return carry

    lax.fori_loop(0, 4, second, 0)

    grad = mm(s["hidden"][...], s["dparams"][...], NT)
    for half in range(2):
        s["ppart"][half] = grad[:, 128 * half : 128 * half + 128].reshape(16, 40, 128)


def entropy_backward(s, pw):
    def third(i, carry):
        lanes = pl.ds(pl.multiple_of(i * 256, 256), 256)
        back = mm(pw[...], s["dparams"][:, lanes])
        s["dpre"][:, lanes] = (back * s["gate"][:, lanes]).astype(BF)
        return carry

    lax.fori_loop(0, 4, third, 0)


def hidden_grads(s):
    hpart = s["hpart"]
    ones = jnp.ones((8, 1024), BF)
    pb = mm(ones, s["dparams"][...], NT)
    grad = mm(s["normed"][0:128, :], s["dpre"][...], NT)
    hb = mm(ones, s["dpre"][...], NT)
    zeros = jnp.zeros((1, 128), F32)
    lines = [hb[0:1, 128 * k : 128 * k + 128] for k in range(5)]
    lines += [pb[0:1, 0:128], pb[0:1, 128:256], zeros]
    for t in range(80):
        core, place, row = tile_spot(t)
        n, k = t // 5, t % 5
        hpart[core, place, row : row + 8] = grad[8 * n : 8 * n + 8, 128 * k : 128 * k + 128]
    hpart[0, 13, 8:16] = jnp.concatenate(lines, axis=0)
    hpart[1, 13, 8:16] = jnp.zeros((8, 128), F32)
    for core in range(2):
        hpart[core, 13, 16:24] = jnp.zeros((8, 128), F32)
        hpart[core, 14:16] = jnp.zeros((2, 24, 128), F32)


def conv_backward(s, hw):
    for level in range(4):
        lanes = slice(256 * level, 256 * level + 256)
        dfeat = mm(hw[...], s["dpre"][:, lanes]).astype(BF).astype(F32)
        dn = jnp.concatenate([dfeat, s["dtargets"][:, lanes].astype(F32)], axis=0)
        inv = s["inv"][:, lanes]
        y = s["conv"][:, lanes]
        dni = dn * inv
        weighted = dni * y * (inv * inv)
        s["dconv"][:, lanes] = (dni - y * mix(s["gamt"], weighted)).astype(BF)


def weight_grads(s):
    for dl in range(3):
        first, last = max(0, 1 - dl), min(4, 5 - dl)
        d = s["dconv"][:, 256 * first : 256 * last]
        x = s["xt"][:, 256 * (first + dl - 1) : 256 * (last + dl - 1)]
        s["taps"][dl] = mm(d, x, NT)
    for dl in range(3):
        for da in range(3):
            n = dl * 3 + da
            for g in range(2):
                total = None
                for p in range(2):
                    row = g * 128 + 2 * p * 32
                    lanes = slice(256 * (da + p), 256 * (da + p) + 256)
                    a = s["taps"][dl, row : row + 32, lanes]
                    b = s["taps"][dl, row + 32 : row + 64, lanes]
                    term = a + pltpu.roll(b, 192, 1)
                    total = term if total is None else total + term
                s["wgrad"][32 * g : 32 * g + 32, 192 * n : 192 * n + 192] = total[:, 0:192]
    s["wgrad"][:, 1728:2048] = jnp.zeros((64, 320), F32)
    lane = iota((8, 128), 1) >> 5
    for k in range(64):
        first = 27 * k
        base = first // 128 * 128
        offset = first - base
        wide = 128 if offset <= 101 else 256
        lon, x = k // 4, k % 4
        core, y, zlo = lon % 2, (lon // 2) % 4, lon // 8
        for g in range(2):
            tile = None
            for q in range(4):
                v = s["wgrad"][32 * g + 8 * q : 32 * g + 8 * q + 8, base : base + wide]
                shift = (32 * q - offset) % wide
                v = pltpu.roll(v, shift, 1)[:, 0:128] if shift else v[:, 0:128]
                tile = v if tile is None else jnp.where(lane == q, v, tile)
            s["cpart"][core, g * 2 + zlo, y, x] = tile


def body(
    x_hbm, cw_hbm, gamma_ref, beta_ref, hw_hbm, hb_ref, pw_hbm, pb_ref,
    ptotal, htotal, cg_ref,
    x, cw, hw, pw, wl, gb,
    own, rim_out, rim_in, field, wall, gall, rims, pick,
    xt, wf, gam, gamt, beta, hwt, pwt, hbt, pbt,
    conv, inv, normed, hidden, gate, dparams, dtargets, dpre, dconv, taps, wgrad,
    ppart, hpart, cpart, pr1, hr1, pr2, hr2, pr3, hr3, q1, q2, q3,
    local_sem, xs, xr, ks, kr, bs, br, es, er, gs, gr, cs, cr,
):
    place = Place()
    lon, lat, chi = place.lon, place.lat, place.ch
    core, z, y = place.core, place.z, place.y
    partner = (lon, lat, 1 - chi)
    sibling = place.sibling()
    other = 1 - chi
    loads = [
        pltpu.make_async_copy(src, dst, local_sem.at[n])
        for n, (src, dst) in enumerate(((x_hbm, x), (cw_hbm, cw), (hw_hbm, hw), (pw_hbm, pw)))
    ]
    for copy in loads:
        copy.start()
    barrier, count = enter(place)
    loads[1].wait()
    pack_weights(cw, gamma_ref, beta_ref, wl, gb)
    loads[0].wait()
    shuffle_latents(x, own, rim_out)
    pl.semaphore_wait(barrier, count)

    mine = pl.ds(pl.multiple_of(16 * core, 16), 16)
    theirs = pl.ds(pl.multiple_of(16 * (1 - core), 16), 16)
    sends = []

    def start(*copies):
        for copy in copies:
            copy.start()
        sends.extend(copies)
        return copies

    def arrive(copies):
        for copy in copies:
            copy.wait_recv()

    start(
        remote(wl.at[mine], wall.at[chi, mine], xs.at[4], xr.at[4], partner),
        remote(gb, gall.at[chi], xs.at[5], xr.at[5], partner),
    )
    down, up = (lat + 3) % 4, (lat + 1) % 4
    for side in range(2):
        near = (lon + 1) % 16 if side == 0 else (lon + 15) % 16
        for kind, (row, half) in enumerate(((lat, 0), (lat, 1), (down, 1), (up, 0))):
            slot = 9 + (side * 2 + kind // 2) * 2
            start(
                remote(
                    rim_out, rim_in.at[side, kind // 2, chi],
                    xs.at[9 + side * 4 + kind], xr.at[slot + chi], (near, row, half),
                )
            )
    start(
        remote(own.at[:, 0], field.at[:, chi, 9], xs.at[7], xr.at[7 + chi], (lon, down, 1)),
        remote(own.at[:, 15], field.at[:, chi, 0], xs.at[8], xr.at[7 + chi], (lon, up, 0)),
    )
    levels = [
        remote(
            own.at[level, pl.ds(7 * other, 9)], field.at[level, chi, pl.ds(chi, 9)],
            xs.at[level], xr.at[level], partner,
        )
        for level in range(4)
    ]
    levels[0].start()
    levels[1].start()
    for level in range(4):
        field[level, chi, pl.ds(other, 9)] = own[level, pl.ds(7 * chi, 9)]
    wall[chi] = wl[...]
    gall[chi] = gb[...]
    loads[2].wait()
    loads[3].wait()
    prepare_small(hw, hb_ref, pw, pb_ref, hwt, pwt, hbt, pbt)
    pick[...] = window_pick()
    remote(gb, gall.at[other], xs.at[5], xr.at[5], partner).wait_recv()
    remote(wl.at[mine], wall.at[other, mine], xs.at[4], xr.at[4], partner).wait_recv()
    start(remote(wall.at[other, mine], wall.at[other, mine], xs.at[6], xr.at[6], sibling))
    levels[0].wait_send()
    levels[2].start()
    build_gamma(gall, gam, gamt, beta)
    levels[1].wait_send()
    levels[3].start()
    for half in range(2):
        remote(
            own.at[:, 0], field.at[:, half, 9 * chi], xs.at[7], xr.at[7 + half], partner
        ).wait_recv()
    for side in range(2):
        for kind in range(2):
            for half in range(2):
                remote(
                    rim_out, rim_in.at[side, kind, half], xs.at[9],
                    xr.at[9 + (side * 2 + kind) * 2 + half], partner,
                ).wait_recv()
    place_rims(place, rim_in, rims)
    remote(
        wall.at[other, mine], wall.at[other, theirs], xs.at[6], xr.at[6], sibling
    ).wait_recv()
    build_weights(wall, wf)

    @pl.when(jnp.where(chi == 0, lat, 3 - lat) == 0)
    def _():
        field[:, :, pl.ds(9 * chi, 1)] = jnp.zeros((4, 2, 1, 32, 128), BF)

    s = {
        "xt": xt, "wf": wf, "gam": gam, "gamt": gamt, "beta": beta, "hwt": hwt, "pwt": pwt,
        "hbt": hbt, "pbt": pbt, "conv": conv, "inv": inv, "normed": normed, "hidden": hidden,
        "gate": gate, "dparams": dparams, "dtargets": dtargets, "dpre": dpre, "dconv": dconv,
        "taps": taps, "wgrad": wgrad, "ppart": ppart, "hpart": hpart, "cpart": cpart,
    }
    for level in range(4):
        remote(
            own.at[level, pl.ds(0, 9)], field.at[level, other, pl.ds(other, 9)],
            xs.at[level], xr.at[level], partner,
        ).wait_recv()
        build_windows(field, rims, pick, xt, level)
        if level >= 1:
            forward(s, level - 1)
    sends.extend(levels[2:])
    forward(s, 3)
    entropy_forward(s)

    parts, totals = (ppart, hpart), (ptotal, htotal)
    firsts, seconds, thirds = (pr1, hr1), (pr2, hr2), (pr3, hr3)

    def core_stage(n):
        return start(
            remote(parts[n].at[1 - core], firsts[n], ks.at[n], kr.at[n], sibling)
        )

    def core_add(n):
        parts[n][core] = parts[n][core] + firsts[n][...]

    def plane_stage(n):
        return start(
            *[
                remote(
                    parts[n].at[core, place.spot(n, a, b)], seconds[n].at[4 * a + b],
                    bs.at[n, 4 * a + b], br.at[n, 4 * a + b], place.plane(n, a, b),
                )
                for a, b in OFFSETS
            ]
        )

    def plane_add(n):
        terms = [parts[n][core, place.spot(n)]] + [seconds[n][k] for k in range(1, 16)]
        while len(terms) > 1:
            terms = [terms[k] + terms[k + 1] for k in range(0, len(terms), 2)]
        thirds[n][place.axis(n)] = terms[0]

    def axis_stage(n):
        axis = place.axis(n)
        copies = start(
            *[
                remote(
                    thirds[n].at[axis], thirds[n].at[axis],
                    es.at[n, d], er.at[n, d], place.along(n, d),
                )
                for d in (1, 2, 3)
            ]
        )
        return [
            remote(
                thirds[n].at[axis], thirds[n].at[(axis + 4 - d) % 4],
                es.at[n, d], er.at[n, d], sibling,
            )
            for d in (1, 2, 3)
        ]

    def axis_add(n):
        totals[n][core, place.spot(n)] = (thirds[n][0] + thirds[n][1]) + (thirds[n][2] + thirds[n][3])

    def spread_stage(n):
        view = totals[n].at[core, place.spot(n)]
        start(
            *[
                remote(
                    view, view, gs.at[n, 4 * a + b], gr.at[n, 4 * a + b], place.plane(n, a, b)
                )
                for a, b in OFFSETS
            ]
        )
        return [
            remote(
                view, totals[n].at[core, place.spot(n, 4 - a, 4 - b)],
                gs.at[n, 4 * a + b], gr.at[n, 4 * a + b], sibling,
            )
            for a, b in OFFSETS
        ]

    def core_spread(n):
        view = totals[n].at[core]
        start(remote(view, view, ks.at[2 + n], kr.at[2 + n], sibling))
        return [remote(view, totals[n].at[1 - core], ks.at[2 + n], kr.at[2 + n], sibling)]

    core_p = core_stage(0)
    entropy_backward(s, pw)
    arrive(core_p)
    core_add(0)
    plane_p = plane_stage(0)
    hidden_grads(s)
    core_h = core_stage(1)
    conv_backward(s, hw)
    arrive(core_h)
    core_add(1)
    plane_h = plane_stage(1)
    weight_grads(s)
    core_c = start(remote(cpart.at[1 - core], q1, cs.at[0], cr.at[0], sibling))
    arrive(plane_p)
    plane_add(0)
    axis_p = axis_stage(0)
    arrive(core_c)
    cpart[core] = cpart[core] + q1[...]
    axis_c = start(
        *[
            remote(
                cpart.at[core, (z + d) % 4], q2.at[d - 1], cs.at[d], cr.at[d], place.along_z(d)
            )
            for d in (1, 2, 3)
        ]
    )
    arrive(plane_h)
    plane_add(1)
    axis_h = axis_stage(1)
    arrive(axis_p)
    axis_add(0)
    spread_p = spread_stage(0)
    arrive(axis_h)
    axis_add(1)
    spread_h = spread_stage(1)
    arrive(axis_c)
    cpart[core, z] = (cpart[core, z] + q2[0]) + (q2[1] + q2[2])
    plane_c = start(
        *[
            remote(
                cpart.at[core, z, (y + b) % 4, (place.x + a) % 4], q3.at[4 * a + b],
                cs.at[3 + 4 * a + b],
                cr.at[3 + 4 * a + b], place.flat(a, b),
            )
            for a, b in OFFSETS
        ]
    )
    arrive(spread_p)
    core_p = core_spread(0)
    arrive(spread_h)
    core_h = core_spread(1)
    arrive(plane_c)
    terms = [cpart[core, z, y, place.x]] + [q3[k] for k in range(1, 16)]
    while len(terms) > 1:
        terms = [terms[k] + terms[k + 1] for k in range(0, len(terms), 2)]
    for q in range(4):
        v = pltpu.roll(terms[0], 128 - 32 * q, 1) if q else terms[0]
        cg_ref[8 * q : 8 * q + 8, :] = v
    arrive(core_p)
    arrive(core_h)
    for copy in sends:
        copy.wait_send()


def unpack(ptotal, htotal, block_ref, cg_ref, hwg_ref, hbg_ref, pwg_ref, pbg_ref):
    cg_ref[...] = block_ref[:, 0:27]
    for half in range(2):
        pwg_ref[:, 128 * half : 128 * half + 128] = ptotal[half].reshape(640, 128)
    for t in range(80):
        core, place, row = tile_spot(t)
        n, k = t // 5, t % 5
        hwg_ref[8 * n : 8 * n + 8, 128 * k : 128 * k + 128] = htotal[core, place, row : row + 8]
    for k in range(5):
        hbg_ref[128 * k : 128 * k + 128] = htotal[0, 13, 8 + k]
    for k in range(2):
        pbg_ref[128 * k : 128 * k + 128] = htotal[0, 13, 13 + k]


def on_device(x, cw, gamma, beta, hw, hb, pw, pb):
    vmem = pltpu.VMEM
    dma = pltpu.SemaphoreType.DMA
    scratch = [
        vmem((4, 32, 16, 128), BF),
        vmem((27, 32, 64), BF),
        vmem((128, 640), BF),
        vmem((640, 256), BF),
        vmem((32, 1792), BF),
        vmem((32, 128), F32),
        vmem((4, 16, 32, 128), BF),
        vmem((32, 128), BF),
        vmem((2, 2, 2, 32, 128), BF),
        vmem((4, 2, 10, 32, 128), BF),
        vmem((2, 32, 1792), BF),
        vmem((2, 32, 128), F32),
        vmem((64, 128), F32),
        vmem((384, 512), BF),
        vmem((1024, 1024), BF),
        vmem((3, 256, 1024), BF),
        vmem((512, 256), BF),
        vmem((512, 256), BF),
        vmem((256, 256), F32),
        vmem((640, 128), BF),
        vmem((256, 640), BF),
        vmem((640, 128), F32),
        vmem((256, 128), F32),
        vmem((256, 1024), F32),
        vmem((256, 1024), F32),
        vmem((256, 1024), BF),
        vmem((640, 1024), BF),
        vmem((640, 1024), F32),
        vmem((256, 1024), BF),
        vmem((128, 1024), BF),
        vmem((640, 1024), BF),
        vmem((256, 1024), BF),
        vmem((3, 256, 1024), F32),
        vmem((64, 2048), F32),
        vmem((2, 16, 40, 128), F32),
        vmem((2, 16, 24, 128), F32),
        vmem((2, 4, 4, 4, 8, 128), F32),
        vmem((16, 40, 128), F32),
        vmem((16, 24, 128), F32),
        vmem((16, 40, 128), F32),
        vmem((16, 24, 128), F32),
        vmem((4, 40, 128), F32),
        vmem((4, 24, 128), F32),
        vmem((4, 4, 4, 8, 128), F32),
        vmem((3, 4, 4, 8, 128), F32),
        vmem((16, 8, 128), F32),
        dma((4,)),
        dma((17,)),
        dma((17,)),
        dma((4,)),
        dma((4,)),
        dma((2, 16)),
        dma((2, 16)),
        dma((2, 4)),
        dma((2, 4)),
        dma((2, 16)),
        dma((2, 16)),
        dma((19,)),
        dma((19,)),
    ]
    spec = pl.BlockSpec(memory_space=pltpu.VMEM)
    anywhere = pl.BlockSpec(memory_space=pl.ANY)
    ptotal, htotal, block = pl.pallas_call(
        body,
        out_shape=(
            jax.ShapeDtypeStruct((2, 16, 40, 128), F32),
            jax.ShapeDtypeStruct((2, 16, 24, 128), F32),
            jax.ShapeDtypeStruct((32, 128), F32),
        ),
        in_specs=[anywhere, anywhere, spec, spec, anywhere, spec, anywhere, spec],
        out_specs=(spec, spec, spec),
        scratch_shapes=scratch,
        compiler_params=pltpu.CompilerParams(
            collective_id=0, has_side_effects=True, vmem_limit_bytes=56 * 1024 * 1024
        ),
    )(x, jnp.transpose(cw, (1, 0, 2)), gamma, beta, hw, hb, pw, pb)
    return pl.pallas_call(
        unpack,
        out_shape=(
            jax.ShapeDtypeStruct((32, 27), F32),
            jax.ShapeDtypeStruct((128, 640), F32),
            jax.ShapeDtypeStruct((640,), F32),
            jax.ShapeDtypeStruct((640, 256), F32),
            jax.ShapeDtypeStruct((256,), F32),
        ),
        in_specs=[spec] * 3,
        out_specs=(spec,) * 5,
    )(ptotal, htotal, block)


def solution(mesh):
    placed = (
        P(None, "ch", "lat", "lon"),
        P("ch", None, None),
        P("ch", None),
        P("ch"),
        P(),
        P(),
        P(),
        P(),
    )
    return jax.shard_map(
        on_device,
        mesh=mesh,
        in_specs=placed,
        out_specs=(P("ch", ("lon", "lat")), P(), P(), P(), P()),
        check_vma=False,
    )
```
